32 devices in a mesh: tiles: 2 (over y), band: 4 (over x, core), head: 4 (over z).
Axes of the slice: x: 2, y: 2, z: 4, core: 2. Of those that a mesh axis runs over, the one named last changes fastest.
Arguments:
- tokens: bfloat16 [8192, 1024], P(('tiles', 'band')), parts along dimension 0, may hold values from -24 to 24
- w_query: bfloat16 [1024, 1024], P(None, 'head'), may hold values from -0.375 to 0.375
- w_key: bfloat16 [1024, 1024], P(None, 'head'), may hold values from -0.1875 to 0.1875
- w_value: bfloat16 [1024, 1024], P(None, 'head'), may hold values from -0.1875 to 0.1875
- w_out: bfloat16 [1024, 1024], P('head'), may hold values from -0.75 to 0.75
- block_mask: int32 [64, 32], P('tiles'), parts along dimension 0, may hold values from 0 to 1, as said below
Outputs:
- projected: bfloat16 [8192, 1024], P(('tiles', 'band', 'head')), parts along dimension 0
The draws below stay inside these ranges and needn't reach their ends.
There are 2 independent parts, one for each index of `tiles`. The reference program is written for one: setup_inputs(seed, part) draws one part's arguments, and reference() takes and returns one part's arrays. A program takes and returns all parts, laid end to end along the dimension named above; an argument that names none is the same for every part. Nothing has to cross between parts.
Inputs may be any that keep to these rules, and one draw needn't show every extreme that they name: `block_mask`: entries are 0 or 1. Every query block may attend to at least one key block. Among the 8 key blocks of one band at most 6 are named by some query block, and some band has exactly 6.
All inputs are finite; a program needn't handle non-finite values.
Results may differ from the reference program's by a relative error of at most 0.02.
Values may be sent and summed in bfloat16 or wider, within the bound.
No kernel may reach another device: no remote copies, remote signals or barrier semaphores. Data moves between devices by JAX's collectives and lax.ppermute only.
A program may use at most 128 MiB of HBM per device.

```python
import math
import jax
import jax.numpy as jnp
from jax import lax

D = 1024
HEADS = 16
HD = 64
BLK = 128
TOK_DEV = 1024
TOKENS = 4096
KEEP = 6


def draw_tokens(key, part):
    first, second = jax.random.split(key, 2)
    base = jax.random.truncated_normal(first, -4.0, 4.0, (TOKENS, D), jnp.float32)
    row_scale = jnp.exp(jax.random.uniform(second, (TOKENS, 1), jnp.float32, math.log(0.7), math.log(1.4)))
    return (base * row_scale).astype(jnp.bfloat16)


def draw_block_mask(key, part):
    block_total = TOKENS // BLK
    per_band = TOK_DEV // BLK
    band_total = TOKENS // TOK_DEV
    streams = jax.random.split(key, 7)
    lowest = (KEEP + 1) // 2
    kept_counts = jax.random.randint(streams[0], (band_total,), lowest, KEEP + 1)
    forced = jax.random.randint(streams[1], (), 0, band_total)
    kept_counts = jnp.where(jnp.arange(band_total) == forced, KEEP, kept_counts)
    raw_order = jax.random.randint(streams[2], (band_total, per_band), 0, 1 << 20) * per_band + jnp.arange(per_band)[None, :]
    block_ranks = jnp.argsort(jnp.argsort(raw_order, axis=1), axis=1)
    has_data = (block_ranks < kept_counts[:, None]).reshape(block_total).astype(jnp.int32)
    levels = jax.random.randint(streams[3], (band_total,), 0, 8)
    percent = 4 + 88 * levels * levels // 49
    band_of_row = jnp.arange(block_total) // per_band
    chance = jax.random.randint(streams[4], (block_total, block_total), 0, 100)
    allowed = (chance < percent[band_of_row][:, None]).astype(jnp.int32) * has_data[None, :]
    pick_raw = (jax.random.randint(streams[5], (block_total, block_total), 0, 1 << 16) * block_total + jnp.arange(block_total)[None, :] + 1) * has_data[None, :]
    picked = jnp.argmax(pick_raw, axis=1)
    allowed = jnp.maximum(allowed, (jnp.arange(block_total)[None, :] == picked[:, None]).astype(jnp.int32))
    row_pick = jax.random.randint(streams[6], (block_total,), 0, block_total)
    column_hits = (jnp.arange(block_total)[:, None] == row_pick[None, :]).astype(jnp.int32) * has_data[None, :]
    allowed = jnp.maximum(allowed, column_hits)
    return allowed.astype(jnp.int32)


def block_levels(stream_key, shape, shards, low, high):
    def one(dim, blocks):
        draws = jax.random.uniform(jax.random.fold_in(jax.random.fold_in(stream_key, 6), dim), (blocks,), jnp.float32, low / len(shards), high / len(shards))
        return jnp.repeat(jnp.exp(draws), shape[dim] // blocks).reshape((-1,) + (1,) * (len(shape) - dim - 1))

    level = one(*shards[0])
    for cut in shards[1:]:
        level = level * one(*cut)
    return level


def scatter_about(rng, dims, width, reach, cuts=(), held_as=jnp.bfloat16):
    level = block_levels(rng, dims, cuts, -0.22, 0.18) if cuts else 1.0
    array = jax.random.normal(rng, dims, jnp.float32) * width * level
    return jnp.minimum(jnp.maximum(array, -reach), reach).astype(held_as)


def setup_inputs(seed: int = 0, part: int = 0) -> dict:
    seeds = jax.random.split(jax.random.key(seed), 7)
    own_keys = jax.random.split(jax.random.fold_in(seeds[6], part), 7)
    return {
        "tokens": draw_tokens(jax.random.fold_in(jax.random.fold_in(seeds[6], part), 71), part),
        "w_query": scatter_about(seeds[1], (D, D), (D // 4) ** -0.5, 0.375, ((1, 4),)),
        "w_key": scatter_about(seeds[2], (D, D), D ** -0.5, 0.1875, ((1, 4),)),
        "w_value": scatter_about(seeds[3], (D, D), D ** -0.5, 0.1875, ((1, 4),)),
        "w_out": scatter_about(seeds[4], (D, D), HD ** -0.5, 0.75, ((0, 4),)),
        "block_mask": draw_block_mask(jax.random.fold_in(jax.random.fold_in(seeds[6], part), 71), part),
    }


def reference(tokens, w_query, w_key, w_value, w_out, block_mask):
    queries = jnp.dot(tokens, w_query, preferred_element_type=jnp.float32).astype(jnp.bfloat16)
    key_rows = jnp.dot(tokens, w_key, preferred_element_type=jnp.float32).astype(jnp.bfloat16)
    value_rows = jnp.dot(tokens, w_value, preferred_element_type=jnp.float32).astype(jnp.bfloat16)
    total_rows = tokens.shape[0]
    block_count = total_rows // BLK
    key_heads = key_rows.astype(jnp.float32).reshape(total_rows, HEADS, HD)
    value_heads = value_rows.astype(jnp.float32).reshape(total_rows, HEADS, HD)
    score_scale = HD ** -0.5

    def one_block(packed):
        query_block, mask_row = packed
        query_heads = query_block.astype(jnp.float32).reshape(BLK, HEADS, HD)
        scores = jnp.einsum("rhd,khd->hrk", query_heads, key_heads, precision=lax.Precision.HIGHEST) * score_scale
        keep_keys = jnp.repeat(mask_row, BLK) > 0
        scores = jnp.where(keep_keys[None, None, :], scores, -jnp.inf)
        row_peak = jnp.max(scores, axis=2, keepdims=True)
        exponent = jnp.where(keep_keys[None, None, :], jnp.exp(scores - row_peak), 0.0)
        row_mass = jnp.sum(exponent, axis=2)
        rounded = lax.optimization_barrier(exponent.astype(jnp.bfloat16)).astype(jnp.float32)
        weighted = jnp.einsum("hrk,khd->rhd", rounded, value_heads, precision=lax.Precision.HIGHEST)
        return (weighted / row_mass.T[:, :, None]).reshape(BLK, HEADS * HD).astype(jnp.bfloat16)

    attended = lax.map(one_block, (queries.reshape(block_count, BLK, HEADS * HD), block_mask))
    attended = attended.reshape(total_rows, HEADS * HD)
    return jnp.dot(attended, w_out, preferred_element_type=jnp.float32).astype(jnp.bfloat16)
```

```python
import functools
import math

import jax
import jax.numpy as jnp
from jax import lax
from jax.experimental import pallas as pl
from jax.experimental.pallas import tpu as pltpu
from jax.sharding import PartitionSpec as P

HD = 64
BLK = 128
KEEP = 6
LANES = 128
NEG = -1e30
LOWEST = -3e38
CHUNK = 512
QUERY_SCALE = HD**-0.5 * math.log2(math.e)
PARAMS = pltpu.CompilerParams(vmem_limit_bytes=56 * 2**20)
ANY = pl.BlockSpec(memory_space=pl.ANY)
VMEM = pl.BlockSpec(memory_space=pltpu.VMEM)


def dot_f32(left, right):
    return jnp.dot(left, right, preferred_element_type=jnp.float32)


def low_lanes(shape):
    return lax.broadcasted_iota(jnp.int32, shape, len(shape) - 1) < HD


def swap_halves(array):
    return pltpu.roll(array, HD, array.ndim - 1)


def project_kv(place, block_mask, tokens, w_key, w_value):
    rows_in, width = tokens.shape
    per_band = rows_in // BLK
    local_cols = w_key.shape[1]
    pairs = local_cols // LANES
    rows = KEEP * BLK
    query_blocks = block_mask.shape[0]

    def kernel(place_ref, mask_ref, tok_ref, wk_ref, wv_ref, *rest):
        outs, (tok, wk, wv, sems) = rest[:pairs], rest[pairs:]
        copies = [
            pltpu.make_async_copy(wk_ref, wk, sems.at[KEEP]),
            pltpu.make_async_copy(wv_ref, wv, sems.at[KEEP + 1]),
        ]
        for copy in copies:
            copy.start()
        first = place_ref[0] * per_band

        def look(i, seen):
            return tuple(s | mask_ref[i, first + j] for j, s in enumerate(seen))

        seen = lax.fori_loop(0, query_blocks, look, (jnp.int32(0),) * per_band, unroll=8)
        order = [jnp.int32(0)] * KEEP
        count = jnp.int32(0)
        for j in range(per_band):
            for e in range(KEEP):
                order[e] = jnp.where((seen[j] > 0) & (count == e), j, order[e])
            count = count + seen[j]
        for e in range(KEEP):
            source = pl.ds(pl.multiple_of(order[e] * BLK, BLK), BLK)
            copy = pltpu.make_async_copy(tok_ref.at[source, :], tok.at[pl.ds(e * BLK, BLK), :], sems.at[e])
            copy.start()
            copies.append(copy)
        for copy in copies:
            copy.wait()
        keys = dot_f32(tok[...], wk[...])
        values = dot_f32(tok[...], wv[...])
        low = low_lanes((rows, LANES))
        for p in range(pairs):
            cols = slice(p * LANES, (p + 1) * LANES)
            k, v = keys[:, cols], values[:, cols]
            outs[p][0] = jnp.where(low, k, swap_halves(v)).astype(jnp.bfloat16)
            outs[p][1] = jnp.where(low, swap_halves(k), v).astype(jnp.bfloat16)

    return pl.pallas_call(
        kernel,
        out_shape=[jax.ShapeDtypeStruct((2, rows, LANES), jnp.bfloat16)] * pairs,
        grid_spec=pltpu.PrefetchScalarGridSpec(
            num_scalar_prefetch=2,
            grid=(),
            in_specs=[ANY, ANY, ANY],
            out_specs=[VMEM] * pairs,
            scratch_shapes=[
                pltpu.VMEM((rows, width), jnp.bfloat16),
                pltpu.VMEM(w_key.shape, jnp.bfloat16),
                pltpu.VMEM(w_value.shape, jnp.bfloat16),
                pltpu.SemaphoreType.DMA((KEEP + 2,)),
            ],
        ),
        compiler_params=PARAMS,
        name="project_kv",
    )(place, block_mask, tokens, w_key, w_value)


def project_q(place, tokens, w_query, parts):
    rows, width = tokens.shape
    pairs = w_query.shape[1] // LANES
    part = rows // parts

    def kernel(place_ref, tok_ref, w_ref, *outs):
        me = place_ref[1]
        for k in range(parts):
            begin = pl.multiple_of((me ^ k) * part, part)
            q = dot_f32(tok_ref[pl.ds(begin, part), :], w_ref[...]) * QUERY_SCALE
            lane = lax.broadcasted_iota(jnp.int32, (part, LANES), 1)
            row = lax.broadcasted_iota(jnp.int32, (part, LANES), 0) + begin
            hot = (lane == HD + row // BLK).astype(jnp.float32)
            at = pl.ds(k * part, part)
            for p in range(pairs):
                pair = q[:, p * LANES : (p + 1) * LANES]
                outs[p][0, at, :] = jnp.where(lane < HD, pair, hot).astype(jnp.bfloat16)
                outs[p][1, at, :] = jnp.where(lane < HD, swap_halves(pair), hot).astype(jnp.bfloat16)

    return pl.pallas_call(
        kernel,
        out_shape=[jax.ShapeDtypeStruct((2, rows, LANES), jnp.bfloat16)] * pairs,
        grid_spec=pltpu.PrefetchScalarGridSpec(
            num_scalar_prefetch=1, grid=(), in_specs=[VMEM, VMEM], out_specs=[VMEM] * pairs
        ),
        compiler_params=PARAMS,
        cost_estimate=pl.CostEstimate(flops=2 * rows * width * w_query.shape[1], bytes_accessed=3 * 2**20, transcendentals=0),
        name="project_q",
    )(place, tokens, w_query)


def attend(queries, sources, bias, parts):
    rows = queries.shape[1]
    part = rows // parts
    held = KEEP * BLK
    total = held * len(sources)

    def kernel(q_ref, bias_ref, *rest):
        srcs = rest[: len(sources)]
        outs = rest[len(sources) : len(sources) + parts]
        table, key_tab, value_tab, sems = rest[len(sources) + parts :]
        copies = []
        for s, src in enumerate(srcs):
            copy = pltpu.make_async_copy(src, table.at[:, pl.ds(s * held, held), :], sems.at[s])
            copy.start()
            copies.append(copy)
        low = low_lanes((BLK, LANES)).astype(jnp.float32).astype(jnp.bfloat16)
        high = (1.0 - low_lanes((BLK, LANES)).astype(jnp.float32)).astype(jnp.bfloat16)
        for s in range(len(srcs)):
            copies[s].wait()
            for e in range(KEEP):
                block = s * KEEP + e
                at = pl.ds(block * BLK, BLK)
                add = jnp.broadcast_to(bias_ref[block : block + 1, :], (BLK, LANES)).astype(jnp.bfloat16)
                for h in range(2):
                    kv = table[h, at, :]
                    key_tab[h, at, :] = kv * low + add
                    value_tab[h, at, :] = kv * high + low
        sums = []
        for h in range(2):
            q = q_ref[h]
            peak = jnp.full((rows, 1), LOWEST, jnp.float32)
            total_sum = jnp.zeros((rows, LANES), jnp.float32)
            for c in range(-(-total // CHUNK)):
                at = pl.ds(c * CHUNK, min(CHUNK, total - c * CHUNK))
                scores = lax.dot_general(
                    q, key_tab[h, at, :], (((1,), (1,)), ((), ())), preferred_element_type=jnp.float32
                )
                new_peak = jnp.maximum(peak, jnp.max(scores, axis=1, keepdims=True))
                weights = jnp.exp2(scores - new_peak).astype(jnp.bfloat16)
                total_sum = total_sum * jnp.exp2(peak - new_peak) + dot_f32(weights, value_tab[h, at, :])
                peak = new_peak
            sums.append(total_sum)
        first, second = sums
        low = low_lanes((rows, LANES))
        top = jnp.where(low, swap_halves(first), second)
        mass = jnp.where(low, first, swap_halves(second))
        out = (top / mass).astype(jnp.bfloat16)
        for k in range(parts):
            outs[k][...] = out[k * part : (k + 1) * part, :]

    return pl.pallas_call(
        kernel,
        out_shape=[jax.ShapeDtypeStruct((part, LANES), jnp.bfloat16)] * parts,
        in_specs=[VMEM, VMEM] + [ANY] * len(sources),
        out_specs=[VMEM] * parts,
        scratch_shapes=[
            pltpu.VMEM((2, total, LANES), jnp.bfloat16),
            pltpu.VMEM((2, total, LANES), jnp.bfloat16),
            pltpu.VMEM((2, total, LANES), jnp.bfloat16),
            pltpu.SemaphoreType.DMA((len(sources),)),
        ],
        compiler_params=PARAMS,
        cost_estimate=pl.CostEstimate(flops=2 * rows * total * 1024, bytes_accessed=8 * 2**20, transcendentals=2 * rows * total),
        name="attend",
    )(queries, bias, *sources)


def project_out(place, attended, w_slots):
    parts, pairs = len(attended), len(attended[0])
    rows = attended[0][0].shape[0]
    slots = len(w_slots)
    piece, width = w_slots[0].shape[1:]
    depth = parts * pairs * LANES

    def kernel(place_ref, *rest):
        parts_in = rest[: parts * pairs]
        w_refs = rest[parts * pairs : parts * pairs + slots]
        out_ref, w, sems = rest[parts * pairs + slots :]
        mine = place_ref[2]
        copies = []
        for s in range(slots):
            for k in range(parts):
                begin = pl.multiple_of(k * pairs * LANES + (mine ^ s) * piece, piece)
                copy = pltpu.make_async_copy(w_refs[s].at[k], w.at[pl.ds(begin, piece), :], sems.at[s * parts + k])
                copy.start()
                copies.append(copy)
        rows_all = jnp.concatenate([ref[...] for ref in parts_in], axis=1)
        for copy in copies:
            copy.wait()
        out_ref[...] = dot_f32(rows_all, w[...]).astype(jnp.bfloat16)

    return pl.pallas_call(
        kernel,
        out_shape=jax.ShapeDtypeStruct((rows, width), jnp.bfloat16),
        grid_spec=pltpu.PrefetchScalarGridSpec(
            num_scalar_prefetch=1,
            grid=(),
            in_specs=[VMEM] * (parts * pairs) + [ANY] * slots,
            out_specs=VMEM,
            scratch_shapes=[
                pltpu.VMEM((depth, width), jnp.bfloat16),
                pltpu.SemaphoreType.DMA((slots * parts,)),
            ],
        ),
        compiler_params=PARAMS,
        name="project_out",
    )(place, *[a for group in attended for a in group], *w_slots)


def score_bias(block_mask, source_bands, bands, per_band, band):
    used = jnp.max(block_mask, axis=0).reshape(bands, per_band)
    rank = jnp.cumsum(used, axis=1) - 1
    slot = jnp.arange(KEEP, dtype=jnp.int32)
    chosen = (used[:, None, :] > 0) & (rank[:, None, :] == slot[None, :, None])
    chosen = jnp.take(chosen, source_bands, axis=0)
    rows = lax.dynamic_slice_in_dim(block_mask, band * per_band, per_band, 0)
    rows = jnp.take(rows.reshape(per_band, bands, per_band), source_bands, axis=1)
    allowed = jnp.any(chosen[:, :, :, None] & (rows.transpose(1, 2, 0)[:, None] > 0), axis=2)
    bias = jnp.where(allowed, 0.0, NEG).astype(jnp.float32).reshape(-1, per_band)
    return jnp.pad(bias, ((0, 0), (HD, LANES - HD - per_band)))


def on_device(sizes, tokens, w_query, w_key, w_value, w_out, block_mask):
    tiles, bands, heads = sizes
    band, head = lax.axis_index("band"), lax.axis_index("head")
    tile = lax.axis_index("tiles")
    per_band = tokens.shape[0] // BLK
    core = band % 2
    quarters = 2 * tiles
    quarter = core * tiles + tile
    place = jnp.stack([band, head, quarter]).astype(jnp.int32)

    def along_band(array, goes_to):
        return lax.ppermute(array, "band", [(i, goes_to(i)) for i in range(bands)])

    def along_head(array, k):
        return lax.ppermute(array, "head", [(i, i ^ k) for i in range(heads)])

    kv = project_kv(place, block_mask, tokens, w_key, w_value)
    pairs = len(kv)
    source_bands = [band, band ^ 1]
    tables = []
    for p in range(pairs):
        own = [kv[p]]
        for r in range(1, bands // 2):
            own.append(along_band(kv[p], lambda i: (i + 2 * r) % bands))
        tables.append([a for o in own for a in (o, along_band(o, lambda i: i ^ 1))])
    for r in range(1, bands // 2):
        far = (band + bands - 2 * r) % bands
        source_bands += [far, far ^ 1]
    queries = project_q(place, tokens, w_query, heads)
    bias = score_bias(block_mask, jnp.stack(source_bands), bands, per_band, band)

    piece = w_out.shape[0] // quarters
    w_mine = lax.dynamic_slice_in_dim(w_out, quarter * piece, piece, 0)
    w_own = jnp.stack([w_mine] + [along_head(w_mine, k) for k in range(1, heads)])
    w_tile = [w_own] + [
        lax.ppermute(w_own, "tiles", [(i, i ^ s) for i in range(tiles)]) for s in range(1, tiles)
    ]
    w_slots = w_tile + [along_band(w, lambda i: i ^ 1) for w in w_tile]

    attended = [[] for _ in range(heads)]
    for p in range(pairs):
        pieces = attend(queries[p], tables[p], bias, heads)
        attended[0].append(pieces[0])
        for k in range(1, heads):
            attended[k].append(along_head(pieces[k], k))
    return project_out(place, attended, w_slots)


def solution(mesh):
    sizes = tuple(mesh.shape[axis] for axis in ("tiles", "band", "head"))
    return jax.shard_map(
        functools.partial(on_device, sizes),
        mesh=mesh,
        in_specs=(
            P(("tiles", "band"), None),
            P(None, "head"),
            P(None, "head"),
            P(None, "head"),
            P("head", None),
            P("tiles", None),
        ),
        out_specs=P(("tiles", "band", "head"), None),
        check_vma=False,
    )
```

```python
import functools
import math

import jax
import jax.numpy as jnp
from jax import lax
from jax.experimental import pallas as pl
from jax.experimental.pallas import tpu as pltpu
from jax.sharding import PartitionSpec as P

HD = 64
BLK = 128
KEEP = 6
LANES = 128
NEG = -1e30
LOWEST = -3e38
HELD = KEEP * BLK
CHUNK = 512
GROUP = 2 * HELD // CHUNK
QUERY_SCALE = HD**-0.5 * math.log2(math.e)
BLK_BITS = 7
BAND_BITS = 3
SMALL = pltpu.CompilerParams(vmem_limit_bytes=16 * 2**20)
FREE = pl.CostEstimate(flops=0, bytes_accessed=0, transcendentals=0)
LARGE = pltpu.CompilerParams(vmem_limit_bytes=60 * 2**20)
PARAMS = pltpu.CompilerParams(vmem_limit_bytes=40 * 2**20)
ANY = pl.BlockSpec(memory_space=pl.ANY)
VMEM = pl.BlockSpec(memory_space=pltpu.VMEM)


def dot_f32(left, right):
    return jnp.dot(left, right, preferred_element_type=jnp.float32)


def low_lanes(shape):
    return lax.broadcasted_iota(jnp.int32, shape, len(shape) - 1) < HD


def swap_halves(array):
    return pltpu.roll(array, HD, array.ndim - 1)


def block_ranks(mask):
    blocks = mask.shape[1]
    used = jnp.max(mask.astype(jnp.float32), axis=0, keepdims=True)
    earlier = lax.broadcasted_iota(jnp.int32, (blocks, blocks), 0)
    later = lax.broadcasted_iota(jnp.int32, (blocks, blocks), 1)
    counts = ((earlier >> BAND_BITS) == (later >> BAND_BITS)) & (earlier < later)
    rank = dot_f32(jnp.broadcast_to(used, (8, blocks)).astype(jnp.bfloat16), counts.astype(jnp.float32).astype(jnp.bfloat16))
    return jnp.broadcast_to(used, (8, blocks)), rank


def slots_of(used, rank, band):
    lane = lax.broadcasted_iota(jnp.int32, used.shape, 1)
    slot = lax.broadcasted_iota(jnp.int32, used.shape, 0).astype(jnp.float32)
    return jnp.where(((lane >> BAND_BITS) == band) & (rank == slot), used, 0.0)


def project_kv(block_mask, tokens, w_key, w_value):
    pairs = w_key.shape[1] // LANES
    rows_in = tokens.shape[0]
    rows = KEEP * BLK
    step = 2 * BLK
    steps = rows_in // step

    def kernel(mask_any, tok_ref, wk_ref, wv_ref, *rest):
        outs, (mask_ref, tok, wk, wv, held, sems, out_sems) = rest[:pairs], rest[pairs:]
        load_mask = pltpu.make_async_copy(mask_any, mask_ref, sems.at[0])
        loads = [pltpu.make_async_copy(wk_ref, wk, sems.at[1]), pltpu.make_async_copy(wv_ref, wv, sems.at[2])]
        for c in range(steps):
            at = pl.ds(c * step, step)
            loads.append(pltpu.make_async_copy(tok_ref.at[at, :], tok.at[at, :], sems.at[3 + c]))
        for copy in [load_mask] + loads:
            copy.start()
        load_mask.wait()
        used, rank = block_ranks(mask_ref[...])
        picked = slots_of(used, rank, lax.axis_index("band"))
        place = (lax.broadcasted_iota(jnp.int32, picked.shape, 1) & (2**BAND_BITS - 1)).astype(jnp.float32)
        digit = lax.broadcasted_iota(jnp.int32, picked.shape, 0)
        scale = (1 << (BAND_BITS * jnp.minimum(digit, KEEP))).astype(jnp.float32)
        code = jnp.sum(jnp.where(digit < KEEP, picked * place * scale, 0.0)).astype(jnp.int32)
        for copy in loads[:2]:
            copy.wait()
        low = low_lanes((step, LANES))
        for c in range(steps):
            at = pl.ds(c * step, step)
            loads[2 + c].wait()
            keys = dot_f32(tok[at, :], wk[...])
            values = dot_f32(tok[at, :], wv[...])
            for p in range(pairs):
                cols = slice(p * LANES, (p + 1) * LANES)
                k, v = keys[:, cols], values[:, cols]
                held[p, 0, at, :] = jnp.where(low, k, swap_halves(v)).astype(jnp.bfloat16)
                held[p, 1, at, :] = jnp.where(low, swap_halves(k), v).astype(jnp.bfloat16)
        stores = []
        for p in range(pairs):
            for e in range(KEEP):
                begin = pl.multiple_of(((code >> (BAND_BITS * e)) & (2**BAND_BITS - 1)) * BLK, BLK)
                copy = pltpu.make_async_copy(
                    held.at[p, :, pl.ds(begin, BLK), :], outs[p].at[:, pl.ds(e * BLK, BLK), :], out_sems.at[p, e]
                )
                copy.start()
                stores.append(copy)
        for copy in stores:
            copy.wait()

    return pl.pallas_call(
        kernel,
        out_shape=[jax.ShapeDtypeStruct((2, rows, LANES), jnp.bfloat16)] * pairs,
        in_specs=[ANY] * 4,
        out_specs=[ANY] * pairs,
        scratch_shapes=[
            pltpu.VMEM(block_mask.shape, jnp.int32),
            pltpu.VMEM(tokens.shape, jnp.bfloat16),
            pltpu.VMEM(w_key.shape, jnp.bfloat16),
            pltpu.VMEM(w_value.shape, jnp.bfloat16),
            pltpu.VMEM((pairs, 2, rows_in, LANES), jnp.bfloat16),
            pltpu.SemaphoreType.DMA((3 + steps,)),
            pltpu.SemaphoreType.DMA((pairs, KEEP)),
        ],
        compiler_params=LARGE,
        cost_estimate=FREE,
        name="project_kv",
    )(block_mask, tokens, w_key, w_value)


class Tables:
    def __init__(self, landing, key_tab, value_tab, sems, refs):
        self.landing, self.key_tab, self.value_tab = landing, key_tab, value_tab
        self.copies = [
            pltpu.make_async_copy(ref, landing.at[:, pl.ds(s * HELD, HELD), :], sems.at[s]) for s, ref in enumerate(refs)
        ]
        for copy in self.copies:
            copy.start()

    def fill(self, bias_ref, first):
        low = low_lanes((BLK, LANES)).astype(jnp.float32).astype(jnp.bfloat16)
        high = (1.0 - low_lanes((BLK, LANES)).astype(jnp.float32)).astype(jnp.bfloat16)
        for s, copy in enumerate(self.copies):
            copy.wait()
            for e in range(KEEP):
                at = pl.ds((s * KEEP + e) * BLK, BLK)
                row = (first + s) * 8 + e
                add = jnp.broadcast_to(bias_ref[row : row + 1, :], (BLK, LANES)).astype(jnp.bfloat16)
                for h in range(2):
                    kv = self.landing[h, at, :]
                    self.key_tab[h, at, :] = kv * low + add
                    self.value_tab[h, at, :] = kv * high + low

    def sweep(self, q, h, peak, total_sum):
        def chunk(begin, carried):
            peak, total_sum = carried
            at = pl.ds(begin, CHUNK)
            scores = lax.dot_general(
                q, self.key_tab[h, at, :], (((1,), (1,)), ((), ())), preferred_element_type=jnp.float32
            )
            new_peak = jnp.maximum(peak, jnp.max(scores, axis=1, keepdims=True))
            weights = jnp.exp2(scores - new_peak).astype(jnp.bfloat16)
            total_sum = total_sum * jnp.exp2(peak - new_peak) + dot_f32(weights, self.value_tab[h, at, :])
            return new_peak, total_sum

        def group(g, carried):
            for c in range(GROUP):
                begin = (g * GROUP + c) * CHUNK
                carried = chunk(begin if isinstance(g, int) else pl.multiple_of(begin, CHUNK), carried)
            return carried

        groups = self.key_tab.shape[1] // (GROUP * CHUNK)
        carried = (peak, total_sum)
        if groups > 2:
            return lax.fori_loop(0, groups, group, carried)
        for g in range(groups):
            carried = group(g, carried)
        return carried


def table_scratch(sources):
    table = pltpu.VMEM((2, sources * HELD, LANES), jnp.bfloat16)
    return [table, table, table, pltpu.SemaphoreType.DMA((sources,))]


def begin_attention(block_mask, tokens, w_query, early, parts, source_bands):
    rows, width = tokens.shape
    pairs = w_query.shape[1] // LANES
    part = rows // parts
    per_band = rows // BLK
    key_blocks = block_mask.shape[1]
    sources = len(source_bands(0))

    def kernel(mask_ref, tok, w, *rest):
        early_refs, rest = rest[: len(early)], rest[len(early) :]
        outs = rest[:pairs]
        bias_ref, state_ref, held, own_rows, out_sems, *scratch = rest[pairs:]
        tables = Tables(*scratch, early_refs)
        me, band = lax.axis_index("head"), lax.axis_index("band")
        own_rows[...] = jnp.zeros(own_rows.shape, jnp.float32)
        first = pl.multiple_of(band * per_band, per_band)
        own_rows[HD : HD + per_band, :] = mask_ref[pl.ds(first, per_band), :].astype(jnp.float32)
        used, rank = block_ranks(mask_ref[...])
        lane8 = lax.broadcasted_iota(jnp.int32, (8, LANES), 1)
        for s, source in enumerate(source_bands(band)):
            allowed = lax.dot_general(
                slots_of(used, rank, source).astype(jnp.bfloat16),
                own_rows[...].astype(jnp.bfloat16),
                (((1,), (1,)), ((), ())),
                preferred_element_type=jnp.float32,
            )
            queried = (lane8 >= HD) & (lane8 < HD + per_band)
            bias_ref[s * 8 : (s + 1) * 8, :] = jnp.where(queried & (allowed < 0.5), NEG, 0.0)
        lane = lax.broadcasted_iota(jnp.int32, (part, LANES), 1)
        row = lax.broadcasted_iota(jnp.int32, (part, LANES), 0)
        stores = []
        for k in range(parts):
            at = pl.ds(k * part, part)
            begin = pl.multiple_of((me ^ k) * part, part)
            q = dot_f32(tok[pl.ds(begin, part), :], w[...]) * QUERY_SCALE
            hot = (lane - HD == ((row + begin) >> BLK_BITS)).astype(jnp.float32)
            for p in range(pairs):
                pair = q[:, p * LANES : (p + 1) * LANES]
                held[p, 0, at, :] = jnp.where(lane < HD, pair, hot).astype(jnp.bfloat16)
                held[p, 1, at, :] = jnp.where(lane < HD, swap_halves(pair), hot).astype(jnp.bfloat16)
        for p in range(pairs):
            copy = pltpu.make_async_copy(held.at[p], outs[p], out_sems.at[p])
            copy.start()
            stores.append(copy)
        tables.fill(bias_ref, 0)
        lane = lax.broadcasted_iota(jnp.int32, (rows, LANES), 1)
        for h in range(2):
            peak, total_sum = tables.sweep(
                held[0, h], h, jnp.full((rows, 1), LOWEST, jnp.float32), jnp.zeros((rows, LANES), jnp.float32)
            )
            state_ref[h] = jnp.where(lane == 1, peak, total_sum)
        for copy in stores:
            copy.wait()

    out = pl.pallas_call(
        kernel,
        out_shape=[jax.ShapeDtypeStruct((2, rows, LANES), jnp.bfloat16)] * pairs
        + [jax.ShapeDtypeStruct((sources * 8, LANES), jnp.float32), jax.ShapeDtypeStruct((2, rows, LANES), jnp.float32)],
        in_specs=[VMEM] * 3 + [ANY] * len(early),
        out_specs=[ANY] * pairs + [VMEM] * 2,
        scratch_shapes=[
            pltpu.VMEM((pairs, 2, rows, LANES), jnp.bfloat16),
            pltpu.VMEM((LANES, key_blocks), jnp.float32),
            pltpu.SemaphoreType.DMA((pairs,)),
        ]
        + table_scratch(len(early)),
        compiler_params=PARAMS,
        cost_estimate=FREE,
        name="begin_attention",
    )(block_mask, tokens, w_query, *early)
    return out[:pairs], out[pairs], out[pairs + 1]


def attend(queries, state, sources, bias, first, parts, cost):
    rows = queries.shape[1]
    part = rows // parts
    states = [] if state is None else [state]

    def kernel(q_ref, bias_ref, *rest):
        state_refs, rest = rest[: len(states)], rest[len(states) :]
        srcs, rest = rest[: len(sources)], rest[len(sources) :]
        outs, scratch = rest[:parts], rest[parts:]
        tables = Tables(*scratch, srcs)
        tables.fill(bias_ref, first)
        lane = lax.broadcasted_iota(jnp.int32, (rows, LANES), 1)
        low = lane < HD
        sums = []
        for h in range(2):
            if states:
                total_sum = state_refs[0][h]
                peak = jnp.max(jnp.where(lane == 1, total_sum, LOWEST), axis=1, keepdims=True)
                total_sum = jnp.where(lane == 1, pltpu.roll(total_sum, 1, 1), total_sum)
            else:
                peak = jnp.full((rows, 1), LOWEST, jnp.float32)
                total_sum = jnp.zeros((rows, LANES), jnp.float32)
            sums.append(tables.sweep(q_ref[h], h, peak, total_sum)[1])
        top = jnp.where(low, swap_halves(sums[0]), sums[1])
        mass = jnp.where(low, sums[0], swap_halves(sums[1]))
        out = (top / mass).astype(jnp.bfloat16)
        for k in range(parts):
            outs[k][...] = out[k * part : (k + 1) * part, :]

    return pl.pallas_call(
        kernel,
        out_shape=[jax.ShapeDtypeStruct((part, LANES), jnp.bfloat16)] * parts,
        in_specs=[VMEM, VMEM] + [VMEM] * len(states) + [ANY] * len(sources),
        out_specs=[VMEM] * parts,
        scratch_shapes=table_scratch(len(sources)),
        compiler_params=PARAMS,
        cost_estimate=pl.CostEstimate(flops=cost, bytes_accessed=0, transcendentals=0),
        name="attend",
    )(queries, bias, *states, *sources)


def assemble(w_mine, w_other, tiles):
    quarters, heads = 2 * tiles, w_mine.shape[1]
    piece, width = w_mine.shape[2:]
    order = [0]
    bit = heads // 2
    while bit:
        order += [bit ^ k for k in order]
        bit //= 2

    def kernel(mine_ref, other_ref, out_ref, sems):
        quarter = (lax.axis_index("band") & 1) * tiles + lax.axis_index("tiles")
        copies = []
        for s in range(quarters):
            ref = other_ref if s >= tiles else mine_ref
            for i, k in enumerate(order):
                begin = pl.multiple_of((quarters * k + (quarter ^ s)) * piece, piece)
                copy = pltpu.make_async_copy(ref.at[s % tiles, i], out_ref.at[pl.ds(begin, piece), :], sems.at[s, i])
                copy.start()
                copies.append(copy)
        for copy in copies:
            copy.wait()

    return pl.pallas_call(
        kernel,
        out_shape=jax.ShapeDtypeStruct((quarters * heads * piece, width), jnp.bfloat16),
        in_specs=[ANY] * 2,
        out_specs=ANY,
        scratch_shapes=[pltpu.SemaphoreType.DMA((quarters, heads))],
        compiler_params=SMALL,
        cost_estimate=FREE,
        name="assemble",
    )(w_mine, w_other)


def project_out(attended, w_full):
    pieces = [a for group in attended for a in group]
    rows, width = pieces[0].shape[0], w_full.shape[1]

    def kernel(*rest):
        w_ref, out_ref = rest[-2:]
        rows_all = jnp.concatenate([ref[...] for ref in rest[:-2]], axis=1)
        out_ref[...] = dot_f32(rows_all, w_ref[...]).astype(jnp.bfloat16)

    return pl.pallas_call(
        kernel,
        out_shape=jax.ShapeDtypeStruct((rows, width), jnp.bfloat16),
        in_specs=[VMEM] * (len(pieces) + 1),
        out_specs=VMEM,
        compiler_params=SMALL,
        cost_estimate=FREE,
        name="project_out",
    )(*pieces, w_full)


def on_device(sizes, tokens, w_query, w_key, w_value, w_out, block_mask):
    tiles, bands, heads = sizes
    hops = range(1, bands // 2)

    def along_band(array, goes_to):
        return lax.ppermute(array, "band", [(i, goes_to(i)) for i in range(bands)])

    def to_sibling(array):
        return along_band(array, lambda i: i ^ 1)

    def along_head(array, k):
        return lax.ppermute(array, "head", [(i, i ^ k) for i in range(heads)])

    def source_bands(band):
        found = [band, band ^ 1]
        for r in hops:
            far = lax.rem(band + bands - 2 * r, bands)
            found += [far, far ^ 1]
        return found

    kv = project_kv(block_mask, tokens, w_key, w_value)
    pairs = len(kv)
    far = [[along_band(one, lambda i: (i + 2 * r) % bands) for r in hops] for one in kv]
    near = [to_sibling(one) for one in kv]

    def widen(held, came, k):
        held = jnp.concatenate([held, came]) if came is not None else held
        return held, along_head(held, k)

    def other_tiles(array):
        return [lax.ppermute(array, "tiles", [(i, i ^ s) for i in range(tiles)]) for s in range(1, tiles)]

    quarter = (lax.axis_index("band") & 1) * tiles + lax.axis_index("tiles")
    piece = w_out.shape[0] // (2 * tiles)
    w_mine = lax.dynamic_slice_in_dim(w_out, quarter * piece, piece, 0)
    w_mine, kv = lax.optimization_barrier((w_mine, kv))
    bit = heads // 2
    w_mine, arriving = widen(w_mine[None], None, bit)
    queries, bias, state = begin_attention(block_mask, tokens, w_query, [kv[0], near[0]], heads, source_bands)
    far[0], queries, arriving = lax.optimization_barrier((far[0], queries, arriving))
    while bit > 1:
        bit //= 2
        w_mine, arriving = widen(w_mine, arriving, bit)

    attended = [[] for _ in range(heads)]
    for p in range(pairs):
        if p > 0:
            far[p], pieces = lax.optimization_barrier((far[p], pieces))
        late = []
        for one in far[p]:
            late += [one, to_sibling(one)]
        if p == 0:
            pieces = attend(queries[0], state, late, bias, 2, heads, 2**33)
            pieces, arriving = lax.optimization_barrier((pieces, arriving))
            w_mine = jnp.concatenate([w_mine, arriving])[None]
            arriving = other_tiles(w_mine)
        else:
            pieces = attend(queries[p], None, [kv[p], near[p]] + late, bias, 0, heads, 0)
            attended, pieces, arriving = lax.optimization_barrier((attended, pieces, arriving))
        attended[0].append(pieces[0])
        for k in range(1, heads):
            attended[k].append(along_head(pieces[k], k))
    w_mine = jnp.concatenate([w_mine] + arriving)
    w_full = assemble(w_mine, to_sibling(w_mine), tiles)
    return project_out(attended, w_full)


def solution(mesh):
    sizes = tuple(mesh.shape[axis] for axis in ("tiles", "band", "head"))
    return jax.shard_map(
        functools.partial(on_device, sizes),
        mesh=mesh,
        in_specs=(
            P(("tiles", "band"), None),
            P(None, "head"),
            P(None, "head"),
            P(None, "head"),
            P("head", None),
            P("tiles", None),
        ),
        out_specs=P(("tiles", "band", "head"), None),
        check_vma=False,
    )
```

```python
import functools
import math

import jax
import jax.numpy as jnp
from jax import lax
from jax.experimental import pallas as pl
from jax.experimental.pallas import tpu as pltpu
from jax.sharding import PartitionSpec as P

HD = 64
BLK = 128
KEEP = 6
LANES = 128
NEG = -1e30
LOWEST = -3e38
HELD = KEEP * BLK
CHUNK = 512
LONG = 2**33
GROUP = 2 * HELD // CHUNK
QUERY_SCALE = HD**-0.5 * math.log2(math.e)
BLK_BITS = 7
BAND_BITS = 3
SMALL = pltpu.CompilerParams(vmem_limit_bytes=16 * 2**20)
FREE = pl.CostEstimate(flops=0, bytes_accessed=0, transcendentals=0)
LARGE = pltpu.CompilerParams(vmem_limit_bytes=60 * 2**20)
PARAMS = pltpu.CompilerParams(vmem_limit_bytes=40 * 2**20)
ANY = pl.BlockSpec(memory_space=pl.ANY)
HBM = pl.BlockSpec(memory_space=pltpu.HBM)
VMEM = pl.BlockSpec(memory_space=pltpu.VMEM)


def dot_f32(left, right):
    return jnp.dot(left, right, preferred_element_type=jnp.float32)


def low_lanes(shape):
    return lax.broadcasted_iota(jnp.int32, shape, len(shape) - 1) < HD


def swap_halves(array):
    return pltpu.roll(array, HD, array.ndim - 1)


def block_ranks(mask):
    blocks = mask.shape[1]
    used = jnp.max(mask.astype(jnp.float32), axis=0, keepdims=True)
    earlier = lax.broadcasted_iota(jnp.int32, (blocks, blocks), 0)
    later = lax.broadcasted_iota(jnp.int32, (blocks, blocks), 1)
    counts = ((earlier >> BAND_BITS) == (later >> BAND_BITS)) & (earlier < later)
    rank = dot_f32(jnp.broadcast_to(used, (8, blocks)).astype(jnp.bfloat16), counts.astype(jnp.float32).astype(jnp.bfloat16))
    return jnp.broadcast_to(used, (8, blocks)), rank


def slots_of(used, rank, band):
    lane = lax.broadcasted_iota(jnp.int32, used.shape, 1)
    slot = lax.broadcasted_iota(jnp.int32, used.shape, 0).astype(jnp.float32)
    return jnp.where(((lane >> BAND_BITS) == band) & (rank == slot), used, 0.0)


def project_kv(block_mask, tokens, w_key, w_value):
    pairs = w_key.shape[1] // LANES
    rows_in = tokens.shape[0]
    rows = KEEP * BLK
    step = 2 * BLK
    steps = tokens.shape[1] // step

    def kernel(mask_any, tok_ref, wk_ref, wv_ref, *rest):
        outs, (mask_ref, tok, wk, wv, keys, values, held, sems, out_sems) = rest[:pairs], rest[pairs:]
        load_mask = pltpu.make_async_copy(mask_any, mask_ref, sems.at[0])
        load_mask.start()
        loads = []
        for c in range(steps):
            at = pl.ds(c * step, step)
            loads += [
                pltpu.make_async_copy(wk_ref.at[at, :], wk.at[at, :], sems.at[1 + 3 * c]),
                pltpu.make_async_copy(wv_ref.at[at, :], wv.at[at, :], sems.at[2 + 3 * c]),
                pltpu.make_async_copy(tok_ref.at[:, at], tok.at[:, at], sems.at[3 + 3 * c]),
            ]
        for copy in loads:
            copy.start()
        load_mask.wait()
        used, rank = block_ranks(mask_ref[...])
        picked = slots_of(used, rank, lax.axis_index("band"))
        place = (lax.broadcasted_iota(jnp.int32, picked.shape, 1) & (2**BAND_BITS - 1)).astype(jnp.float32)
        digit = lax.broadcasted_iota(jnp.int32, picked.shape, 0)
        scale = (1 << (BAND_BITS * jnp.minimum(digit, KEEP))).astype(jnp.float32)
        code = jnp.sum(jnp.where(digit < KEEP, picked * place * scale, 0.0)).astype(jnp.int32)
        low = low_lanes((rows_in, LANES))
        for c in range(steps):
            at = pl.ds(c * step, step)
            for copy in loads[3 * c : 3 * c + 3]:
                copy.wait()
            for total, weight in ((keys, wk), (values, wv)):
                product = dot_f32(tok[:, at], weight[at, :])
                if c == 0:
                    total[...] = product
                else:
                    total[...] += product
        for p in range(pairs):
            cols = slice(p * LANES, (p + 1) * LANES)
            k, v = keys[:, cols], values[:, cols]
            held[p, 0] = jnp.where(low, k, swap_halves(v)).astype(jnp.bfloat16)
            held[p, 1] = jnp.where(low, swap_halves(k), v).astype(jnp.bfloat16)
        stores = []
        for p in range(pairs):
            for e in range(KEEP):
                begin = pl.multiple_of(((code >> (BAND_BITS * e)) & (2**BAND_BITS - 1)) * BLK, BLK)
                copy = pltpu.make_async_copy(
                    held.at[p, :, pl.ds(begin, BLK), :], outs[p].at[:, pl.ds(e * BLK, BLK), :], out_sems.at[p, e]
                )
                copy.start()
                stores.append(copy)
        for copy in stores:
            copy.wait()

    return pl.pallas_call(
        kernel,
        out_shape=[jax.ShapeDtypeStruct((2, rows, LANES), jnp.bfloat16)] * pairs,
        in_specs=[ANY] * 4,
        out_specs=[ANY] * pairs,
        scratch_shapes=[
            pltpu.VMEM(block_mask.shape, jnp.int32),
            pltpu.VMEM(tokens.shape, jnp.bfloat16),
            pltpu.VMEM(w_key.shape, jnp.bfloat16),
            pltpu.VMEM(w_value.shape, jnp.bfloat16),
            pltpu.VMEM((rows_in, w_key.shape[1]), jnp.float32),
            pltpu.VMEM((rows_in, w_key.shape[1]), jnp.float32),
            pltpu.VMEM((pairs, 2, rows_in, LANES), jnp.bfloat16),
            pltpu.SemaphoreType.DMA((1 + 3 * steps,)),
            pltpu.SemaphoreType.DMA((pairs, KEEP)),
        ],
        compiler_params=LARGE,
        cost_estimate=FREE,
        name="project_kv",
    )(block_mask, tokens, w_key, w_value)


class Tables:
    def __init__(self, landing, key_tab, value_tab, sems, refs):
        self.landing, self.key_tab, self.value_tab = landing, key_tab, value_tab
        self.copies = [
            pltpu.make_async_copy(ref, landing.at[:, pl.ds(s * HELD, HELD), :], sems.at[s]) for s, ref in enumerate(refs)
        ]
        for copy in self.copies:
            copy.start()

    def fill(self, bias_ref, first):
        low = low_lanes((BLK, LANES)).astype(jnp.float32).astype(jnp.bfloat16)
        high = (1.0 - low_lanes((BLK, LANES)).astype(jnp.float32)).astype(jnp.bfloat16)
        for s, copy in enumerate(self.copies):
            copy.wait()
            for e in range(KEEP):
                at = pl.ds((s * KEEP + e) * BLK, BLK)
                row = (first + s) * 8 + e
                add = jnp.broadcast_to(bias_ref[row : row + 1, :], (BLK, LANES)).astype(jnp.bfloat16)
                for h in range(2):
                    kv = self.landing[h, at, :]
                    self.key_tab[h, at, :] = kv * low + add
                    self.value_tab[h, at, :] = kv * high + low

    def sweep(self, q, h, peak, total_sum):
        def chunk(begin, carried):
            peak, total_sum = carried
            at = pl.ds(begin, CHUNK)
            scores = lax.dot_general(
                q, self.key_tab[h, at, :], (((1,), (1,)), ((), ())), preferred_element_type=jnp.float32
            )
            new_peak = jnp.maximum(peak, jnp.max(scores, axis=1, keepdims=True))
            weights = jnp.exp2(scores - new_peak).astype(jnp.bfloat16)
            total_sum = total_sum * jnp.exp2(peak - new_peak) + dot_f32(weights, self.value_tab[h, at, :])
            return new_peak, total_sum

        def group(g, carried):
            for c in range(GROUP):
                begin = (g * GROUP + c) * CHUNK
                carried = chunk(begin if isinstance(g, int) else pl.multiple_of(begin, CHUNK), carried)
            return carried

        groups = self.key_tab.shape[1] // (GROUP * CHUNK)
        carried = (peak, total_sum)
        if groups > 2:
            return lax.fori_loop(0, groups, group, carried)
        for g in range(groups):
            carried = group(g, carried)
        return carried


def table_scratch(sources):
    table = pltpu.VMEM((2, sources * HELD, LANES), jnp.bfloat16)
    return [table, table, table, pltpu.SemaphoreType.DMA((sources,))]


def begin_attention(block_mask, tokens, w_query, early, parts, source_bands):
    rows, width = tokens.shape
    pairs = w_query.shape[1] // LANES
    part = rows // parts
    per_band = rows // BLK
    key_blocks = block_mask.shape[1]
    sources = len(source_bands(0))

    def kernel(mask_ref, tok, w, *rest):
        early_refs, rest = rest[: len(early)], rest[len(early) :]
        outs = rest[:pairs]
        bias_ref, state_ref, held, own_rows, out_sems, *scratch = rest[pairs:]
        tables = Tables(*scratch, early_refs)
        me, band = lax.axis_index("head"), lax.axis_index("band")
        own_rows[...] = jnp.zeros(own_rows.shape, jnp.float32)
        first = pl.multiple_of(band * per_band, per_band)
        own_rows[HD : HD + per_band, :] = mask_ref[pl.ds(first, per_band), :].astype(jnp.float32)
        used, rank = block_ranks(mask_ref[...])
        lane8 = lax.broadcasted_iota(jnp.int32, (8, LANES), 1)
        for s, source in enumerate(source_bands(band)):
            allowed = lax.dot_general(
                slots_of(used, rank, source).astype(jnp.bfloat16),
                own_rows[...].astype(jnp.bfloat16),
                (((1,), (1,)), ((), ())),
                preferred_element_type=jnp.float32,
            )
            queried = (lane8 >= HD) & (lane8 < HD + per_band)
            bias_ref[s * 8 : (s + 1) * 8, :] = jnp.where(queried & (allowed < 0.5), NEG, 0.0)
        lane = lax.broadcasted_iota(jnp.int32, (part, LANES), 1)
        row = lax.broadcasted_iota(jnp.int32, (part, LANES), 0)
        stores = []
        for k in range(parts):
            at = pl.ds(k * part, part)
            begin = pl.multiple_of((me ^ k) * part, part)
            q = dot_f32(tok[pl.ds(begin, part), :], w[...]) * QUERY_SCALE
            hot = (lane - HD == ((row + begin) >> BLK_BITS)).astype(jnp.float32)
            for p in range(pairs):
                pair = q[:, p * LANES : (p + 1) * LANES]
                held[p, 0, at, :] = jnp.where(lane < HD, pair, hot).astype(jnp.bfloat16)
                held[p, 1, at, :] = jnp.where(lane < HD, swap_halves(pair), hot).astype(jnp.bfloat16)
        for p in range(pairs):
            copy = pltpu.make_async_copy(held.at[p], outs[p], out_sems.at[p])
            copy.start()
            stores.append(copy)
        tables.fill(bias_ref, 0)
        lane = lax.broadcasted_iota(jnp.int32, (rows, LANES), 1)
        for h in range(2):
            peak, total_sum = tables.sweep(
                held[0, h], h, jnp.full((rows, 1), LOWEST, jnp.float32), jnp.zeros((rows, LANES), jnp.float32)
            )
            state_ref[h] = jnp.where(lane == 1, peak, total_sum)
        for copy in stores:
            copy.wait()

    out = pl.pallas_call(
        kernel,
        out_shape=[jax.ShapeDtypeStruct((2, rows, LANES), jnp.bfloat16)] * pairs
        + [jax.ShapeDtypeStruct((sources * 8, LANES), jnp.float32), jax.ShapeDtypeStruct((2, rows, LANES), jnp.float32)],
        in_specs=[VMEM] * 3 + [HBM] * len(early),
        out_specs=[ANY] * pairs + [VMEM] * 2,
        scratch_shapes=[
            pltpu.VMEM((pairs, 2, rows, LANES), jnp.bfloat16),
            pltpu.VMEM((LANES, key_blocks), jnp.float32),
            pltpu.SemaphoreType.DMA((pairs,)),
        ]
        + table_scratch(len(early)),
        compiler_params=PARAMS,
        cost_estimate=FREE,
        name="begin_attention",
    )(block_mask, tokens, w_query, *early)
    return out[:pairs], out[pairs], out[pairs + 1]


def attend(queries, state, sources, bias, first, parts, begin, count, cost):
    part = queries.shape[1] // parts
    rows = count * part
    states = [] if state is None else [state]

    def kernel(q_ref, bias_ref, *rest):
        state_refs, rest = rest[: len(states)], rest[len(states) :]
        srcs, rest = rest[: len(sources)], rest[len(sources) :]
        outs, scratch = rest[:count], rest[count:]
        tables = Tables(*scratch, srcs)
        tables.fill(bias_ref, first)
        lane = lax.broadcasted_iota(jnp.int32, (rows, LANES), 1)
        low = lane < HD
        taken = slice(begin * part, begin * part + rows)
        sums = []
        for h in range(2):
            if states:
                total_sum = state_refs[0][h, taken]
                peak = jnp.max(jnp.where(lane == 1, total_sum, LOWEST), axis=1, keepdims=True)
                total_sum = jnp.where(lane == 1, pltpu.roll(total_sum, 1, 1), total_sum)
            else:
                peak = jnp.full((rows, 1), LOWEST, jnp.float32)
                total_sum = jnp.zeros((rows, LANES), jnp.float32)
            sums.append(tables.sweep(q_ref[h, taken], h, peak, total_sum)[1])
        top = jnp.where(low, swap_halves(sums[0]), sums[1])
        mass = jnp.where(low, sums[0], swap_halves(sums[1]))
        out = (top / mass).astype(jnp.bfloat16)
        for k in range(count):
            outs[k][...] = out[k * part : (k + 1) * part, :]

    return pl.pallas_call(
        kernel,
        out_shape=[jax.ShapeDtypeStruct((part, LANES), jnp.bfloat16)] * count,
        in_specs=[VMEM, VMEM] + [VMEM] * len(states) + [HBM] * len(sources),
        out_specs=[VMEM] * count,
        scratch_shapes=table_scratch(len(sources)),
        compiler_params=PARAMS,
        cost_estimate=pl.CostEstimate(flops=cost, bytes_accessed=0, transcendentals=0),
        name="attend",
    )(queries, bias, *states, *sources)


def project_out(attended, w_mine, w_other, tiles):
    heads, depth, width = w_mine.shape
    pairs = len(attended[0])
    rows = attended[0][0].shape[0]
    piece = depth // tiles
    order = [0]
    bit = heads // 2
    while bit:
        order += [bit ^ k for k in order]
        bit //= 2
    pieces = [attended[k][p] for k in order for p in range(pairs)]
    direct = depth % LANES == 0

    def kernel(*rest):
        refs, (mine_ref, other_ref, out_ref, *scratch) = rest[: heads * pairs], rest[heads * pairs :]
        quarter = (lax.axis_index("band") & 1) * tiles + lax.axis_index("tiles")
        lane = lax.broadcasted_iota(jnp.int32, (rows, LANES), 1)
        groups = []
        for i in range(heads):
            group = [refs[i * pairs + p][...].astype(jnp.float32) for p in range(pairs)]
            size = piece
            while size < depth * 2:
                flip = (quarter & (size // piece)) > 0
                if size < LANES:
                    moved = [
                        jnp.where((lane & size) > 0, pltpu.roll(x, size, 1), pltpu.roll(x, LANES - size, 1)) for x in group
                    ]
                else:
                    moved = [group[p ^ (size // LANES)] for p in range(pairs)]
                group = [jnp.where(flip, m, x) for m, x in zip(moved, group)]
                size *= 2
            groups.append([x.astype(jnp.bfloat16) for x in group])
        if direct:
            half = depth // LANES
            near_cols = jnp.concatenate([x for group in groups for x in group[:half]], axis=1)
            far_cols = jnp.concatenate([x for group in groups for x in group[half:]], axis=1)
            total = dot_f32(near_cols, mine_ref[...].reshape(heads * depth, width))
            total += dot_f32(far_cols, other_ref[...].reshape(heads * depth, width))
        else:
            w, sems = scratch
            copies = [
                pltpu.make_async_copy(ref, w.at[:, pl.ds(s * depth, depth), :], sems.at[s])
                for s, ref in enumerate((mine_ref, other_ref))
            ]
            for copy in copies:
                copy.start()
            for copy in copies:
                copy.wait()
            cols = jnp.concatenate([x for group in groups for x in group], axis=1)
            total = dot_f32(cols, w[...].reshape(heads * 2 * depth, width))
        out_ref[...] = total.astype(jnp.bfloat16)

    scratch = [] if direct else [pltpu.VMEM((heads, 2 * depth, width), jnp.bfloat16), pltpu.SemaphoreType.DMA((2,))]
    return pl.pallas_call(
        kernel,
        out_shape=jax.ShapeDtypeStruct((rows, width), jnp.bfloat16),
        in_specs=[VMEM] * len(pieces) + [VMEM if direct else ANY] * 2,
        out_specs=VMEM,
        scratch_shapes=scratch,
        compiler_params=SMALL,
        cost_estimate=FREE,
        name="project_out",
    )(*pieces, w_mine, w_other)


def on_device(sizes, tokens, w_query, w_key, w_value, w_out, block_mask):
    tiles, bands, heads = sizes
    hops = range(1, bands // 2)

    def along_band(array, goes_to):
        return lax.ppermute(array, "band", [(i, goes_to(i)) for i in range(bands)])

    def to_sibling(array):
        return along_band(array, lambda i: i ^ 1)

    def along_head(array, k):
        return lax.ppermute(array, "head", [(i, i ^ k) for i in range(heads)])

    def source_bands(band):
        found = [band, band ^ 1]
        for r in hops:
            far = lax.rem(band + bands - 2 * r, bands)
            found += [far, far ^ 1]
        return found

    kv = project_kv(block_mask, tokens, w_key, w_value)
    pairs = len(kv)
    far = [[along_band(one, lambda i: (i + 2 * r) % bands) for r in hops] for one in kv]
    near = [to_sibling(one) for one in kv]

    def widen(held, came, k):
        held = jnp.concatenate([held, came]) if came is not None else held
        return held, along_head(held, k)

    def other_tiles(array):
        return [lax.ppermute(array, "tiles", [(i, i ^ s) for i in range(tiles)]) for s in range(1, tiles)]

    quarter = (lax.axis_index("band") & 1) * tiles + lax.axis_index("tiles")
    piece = w_out.shape[0] // (2 * tiles)
    w_mine = lax.dynamic_slice_in_dim(w_out, quarter * piece, piece, 0)
    w_mine, kv = lax.optimization_barrier((w_mine, kv))
    bit = heads // 2
    w_mine, arriving = widen(w_mine[None], None, bit)
    queries, bias, state = begin_attention(block_mask, tokens, w_query, [kv[0], near[0]], heads, source_bands)
    far[0], queries, arriving = lax.optimization_barrier((far[0], queries, arriving))
    while bit > 1:
        bit //= 2
        w_mine, arriving = widen(w_mine, arriving, bit)

    attended = [[] for _ in range(heads)]

    def exchange(pieces, first):
        for k, piece in enumerate(pieces, first):
            attended[k].append(piece if k == 0 else along_head(piece, k))

    last = pairs - 1
    if last == 0:
        w_mine = jnp.concatenate([w_mine, arriving])
        arriving = other_tiles(w_mine)
    for p in range(pairs):
        if p > 0:
            far[p], pieces = lax.optimization_barrier((far[p], pieces))
        sources = [] if p == 0 else [kv[p], near[p]]
        for one in far[p]:
            sources += [one, to_sibling(one)]
        held, first = (state, 2) if p == 0 else (None, 0)
        if p < last:
            pieces = attend(queries[p], held, sources, bias, first, heads, 0, heads, LONG)
            if p == 0:
                pieces, arriving = lax.optimization_barrier((pieces, arriving))
                w_mine = jnp.concatenate([w_mine, arriving])
                arriving = other_tiles(w_mine)
            exchange(pieces, 0)
        else:
            pieces = attend(queries[p], held, sources, bias, first, heads, 1, heads - 1, 0)
            pieces, attended, arriving, sources[-1] = lax.optimization_barrier((pieces, attended, arriving, sources[-1]))
            exchange(pieces, 1)
            exchange(attend(queries[p], held, sources, bias, first, heads, 0, 1, LONG), 0)
    w_mine = jnp.concatenate([w_mine] + arriving, axis=1)
    return project_out(attended, w_mine, to_sibling(w_mine), tiles)


def solution(mesh):
    sizes = tuple(mesh.shape[axis] for axis in ("tiles", "band", "head"))
    return jax.shard_map(
        functools.partial(on_device, sizes),
        mesh=mesh,
        in_specs=(
            P(("tiles", "band"), None),
            P(None, "head"),
            P(None, "head"),
            P(None, "head"),
            P("head", None),
            P("tiles", None),
        ),
        out_specs=P(("tiles", "band", "head"), None),
        check_vma=False,
    )
```

```python
import functools
import math

import jax
import jax.numpy as jnp
from jax import lax
from jax.experimental import pallas as pl
from jax.experimental.pallas import tpu as pltpu
from jax.sharding import PartitionSpec as P

HD = 64
BLK = 128
KEEP = 6
LANES = 128
NEG = -1e30
LOWEST = -3e38
HELD = KEEP * BLK
CHUNK = 1536
LONG = 2**33
GROUP = 2 * HELD // CHUNK
QUERY_SCALE = HD**-0.5 * math.log2(math.e)
BLK_BITS = 7
BAND_BITS = 3
SMALL = pltpu.CompilerParams(vmem_limit_bytes=16 * 2**20)
FREE = pl.CostEstimate(flops=0, bytes_accessed=0, transcendentals=0)
LARGE = pltpu.CompilerParams(vmem_limit_bytes=60 * 2**20)
PARAMS = pltpu.CompilerParams(vmem_limit_bytes=32 * 2**20)
ANY = pl.BlockSpec(memory_space=pl.ANY)
HBM = pl.BlockSpec(memory_space=pltpu.HBM)
VMEM = pl.BlockSpec(memory_space=pltpu.VMEM)


def dot_f32(left, right):
    return jnp.dot(left, right, preferred_element_type=jnp.float32)


def low_lanes(shape):
    return lax.broadcasted_iota(jnp.int32, shape, len(shape) - 1) < HD


def swap_halves(array):
    return pltpu.roll(array, HD, array.ndim - 1)


def block_ranks(mask):
    blocks = mask.shape[1]
    used = jnp.max(mask.astype(jnp.float32), axis=0, keepdims=True)
    earlier = lax.broadcasted_iota(jnp.int32, (blocks, blocks), 0)
    later = lax.broadcasted_iota(jnp.int32, (blocks, blocks), 1)
    counts = ((earlier >> BAND_BITS) == (later >> BAND_BITS)) & (earlier < later)
    rank = dot_f32(jnp.broadcast_to(used, (8, blocks)).astype(jnp.bfloat16), counts.astype(jnp.float32).astype(jnp.bfloat16))
    return jnp.broadcast_to(used, (8, blocks)), rank


def slots_of(used, rank, band):
    lane = lax.broadcasted_iota(jnp.int32, used.shape, 1)
    slot = lax.broadcasted_iota(jnp.int32, used.shape, 0).astype(jnp.float32)
    return jnp.where(((lane >> BAND_BITS) == band) & (rank == slot), used, 0.0)


def project_kv(block_mask, tokens, w_key, w_value):
    pairs = w_key.shape[1] // LANES
    rows_in = tokens.shape[0]
    rows = KEEP * BLK
    step = 2 * BLK
    steps = tokens.shape[1] // step

    def kernel(mask_any, tok_ref, wk_ref, wv_ref, *rest):
        outs, rest = rest[: pairs + 1], rest[pairs + 1 :]
        (mask_ref, tok, wk, wv, keys, values, held, sems, out_sems) = rest
        load_mask = pltpu.make_async_copy(mask_any, mask_ref, sems.at[0])
        load_mask.start()
        loads = []
        for c in range(steps):
            at = pl.ds(c * step, step)
            loads += [
                pltpu.make_async_copy(wk_ref.at[at, :], wk.at[at, :], sems.at[1 + 3 * c]),
                pltpu.make_async_copy(wv_ref.at[at, :], wv.at[at, :], sems.at[2 + 3 * c]),
                pltpu.make_async_copy(tok_ref.at[:, at], tok.at[:, at], sems.at[3 + 3 * c]),
            ]
        for copy in loads:
            copy.start()
        load_mask.wait()
        used, rank = block_ranks(mask_ref[...])
        picked = slots_of(used, rank, lax.axis_index("band"))
        place = (lax.broadcasted_iota(jnp.int32, picked.shape, 1) & (2**BAND_BITS - 1)).astype(jnp.float32)
        digit = lax.broadcasted_iota(jnp.int32, picked.shape, 0)
        scale = (1 << (BAND_BITS * jnp.minimum(digit, KEEP))).astype(jnp.float32)
        code = jnp.sum(jnp.where(digit < KEEP, picked * place * scale, 0.0)).astype(jnp.int32)
        low = low_lanes((rows_in, LANES))
        for c in range(steps):
            at = pl.ds(c * step, step)
            for copy in loads[3 * c : 3 * c + 3]:
                copy.wait()
            for total, weight in ((keys, wk), (values, wv)):
                product = dot_f32(tok[:, at], weight[at, :])
                if c == 0:
                    total[...] = product
                else:
                    total[...] += product
        for p in range(pairs):
            cols = slice(p * LANES, (p + 1) * LANES)
            k, v = keys[:, cols], values[:, cols]
            held[p, 0] = jnp.where(low, k, swap_halves(v)).astype(jnp.bfloat16)
            held[p, 1] = jnp.where(low, swap_halves(k), v).astype(jnp.bfloat16)
        stores = []
        for p in range(pairs):
            for e in range(KEEP):
                begin = pl.multiple_of(((code >> (BAND_BITS * e)) & (2**BAND_BITS - 1)) * BLK, BLK)
                block, at = pl.ds(begin, BLK), pl.ds(e * BLK, BLK)
                if p == 0:
                    moves = [(held.at[0, h, block, :], outs[h].at[at, :]) for h in range(2)]
                else:
                    moves = [(held.at[p, :, block, :], outs[p + 1].at[:, at, :])]
                for i, (source, to) in enumerate(moves):
                    copy = pltpu.make_async_copy(source, to, out_sems.at[p, e, i])
                    copy.start()
                    stores.append(copy)
        for copy in stores:
            copy.wait()

    return pl.pallas_call(
        kernel,
        out_shape=[jax.ShapeDtypeStruct((rows, LANES), jnp.bfloat16)] * 2
        + [jax.ShapeDtypeStruct((2, rows, LANES), jnp.bfloat16)] * (pairs - 1),
        in_specs=[ANY] * 4,
        out_specs=[ANY] * (pairs + 1),
        scratch_shapes=[
            pltpu.VMEM(block_mask.shape, jnp.int32),
            pltpu.VMEM(tokens.shape, jnp.bfloat16),
            pltpu.VMEM(w_key.shape, jnp.bfloat16),
            pltpu.VMEM(w_value.shape, jnp.bfloat16),
            pltpu.VMEM((rows_in, w_key.shape[1]), jnp.float32),
            pltpu.VMEM((rows_in, w_key.shape[1]), jnp.float32),
            pltpu.VMEM((pairs, 2, rows_in, LANES), jnp.bfloat16),
            pltpu.SemaphoreType.DMA((1 + 3 * steps,)),
            pltpu.SemaphoreType.DMA((pairs, KEEP, 2)),
        ],
        compiler_params=LARGE,
        cost_estimate=FREE,
        name="project_kv",
    )(block_mask, tokens, w_key, w_value)


class Tables:
    def __init__(self, landing, key_tab, value_tab, sems, refs):
        self.landing, self.key_tab, self.value_tab = landing, key_tab, value_tab
        self.copies = []
        for s, ref in enumerate(refs):
            at = pl.ds(s // 2 * HELD, HELD) if len(ref.shape) == 2 else pl.ds(s * HELD, HELD)
            to = landing.at[s % 2, at, :] if len(ref.shape) == 2 else landing.at[:, at, :]
            self.copies.append(pltpu.make_async_copy(ref, to, sems.at[s]))
        for copy in self.copies:
            copy.start()

    def fill(self, bias_ref, first):
        low = low_lanes((BLK, LANES)).astype(jnp.float32).astype(jnp.bfloat16)
        high = (1.0 - low_lanes((BLK, LANES)).astype(jnp.float32)).astype(jnp.bfloat16)
        sources = self.landing.shape[1] // HELD
        split = len(self.copies) // sources
        for s in range(sources):
            for copy in self.copies[s * split : (s + 1) * split]:
                copy.wait()
            for e in range(KEEP):
                at = pl.ds((s * KEEP + e) * BLK, BLK)
                row = (first + s) * 8 + e
                add = jnp.broadcast_to(bias_ref[row : row + 1, :], (BLK, LANES)).astype(jnp.bfloat16)
                for h in range(2):
                    kv = self.landing[h, at, :]
                    self.key_tab[h, at, :] = kv * low + add
                    self.value_tab[h, at, :] = kv * high + low

    def sweep(self, q, h, peak, total_sum):
        def chunk(begin, carried):
            peak, total_sum = carried
            at = pl.ds(begin, CHUNK)
            scores = lax.dot_general(
                q, self.key_tab[h, at, :], (((1,), (1,)), ((), ())), preferred_element_type=jnp.float32
            )
            new_peak = jnp.maximum(peak, jnp.max(scores, axis=1, keepdims=True))
            weights = jnp.exp2(scores - new_peak).astype(jnp.bfloat16)
            total_sum = total_sum * jnp.exp2(peak - new_peak) + dot_f32(weights, self.value_tab[h, at, :])
            return new_peak, total_sum

        def group(g, carried):
            for c in range(GROUP):
                begin = (g * GROUP + c) * CHUNK
                carried = chunk(begin if isinstance(g, int) else pl.multiple_of(begin, CHUNK), carried)
            return carried

        groups = self.key_tab.shape[1] // (GROUP * CHUNK)
        carried = (peak, total_sum)
        if groups > 2:
            return lax.fori_loop(0, groups, group, carried)
        for g in range(groups):
            carried = group(g, carried)
        return carried


def table_scratch(arrays):
    sources = sum(array.ndim - 1 for array in arrays) // 2
    table = pltpu.VMEM((2, sources * HELD, LANES), jnp.bfloat16)
    return [table, table, table, pltpu.SemaphoreType.DMA((len(arrays),))]


def begin_attention(block_mask, tokens, w_query, early, parts, source_bands):
    rows, width = tokens.shape
    pairs = w_query.shape[1] // LANES
    part = rows // parts
    per_band = rows // BLK
    key_blocks = block_mask.shape[1]
    sources = len(source_bands(0))

    def kernel(mask_ref, tok, w_any, *rest):
        early_refs, rest = rest[: len(early)], rest[len(early) :]
        outs = rest[:pairs]
        bias_ref, state_ref, held, own_rows, w, w_sem, out_sems, *scratch = rest[pairs:]
        load_w = pltpu.make_async_copy(w_any, w, w_sem)
        load_w.start()
        tables = Tables(*scratch, early_refs)
        me, band = lax.axis_index("head"), lax.axis_index("band")
        own_rows[...] = jnp.zeros(own_rows.shape, jnp.float32)
        first = pl.multiple_of(band * per_band, per_band)
        own_rows[HD : HD + per_band, :] = mask_ref[pl.ds(first, per_band), :].astype(jnp.float32)
        used, rank = block_ranks(mask_ref[...])
        lane8 = lax.broadcasted_iota(jnp.int32, (8, LANES), 1)
        for s, source in enumerate(source_bands(band)):
            allowed = lax.dot_general(
                slots_of(used, rank, source).astype(jnp.bfloat16),
                own_rows[...].astype(jnp.bfloat16),
                (((1,), (1,)), ((), ())),
                preferred_element_type=jnp.float32,
            )
            queried = (lane8 >= HD) & (lane8 < HD + per_band)
            bias_ref[s * 8 : (s + 1) * 8, :] = jnp.where(queried & (allowed < 0.5), NEG, 0.0)
        load_w.wait()
        lane = lax.broadcasted_iota(jnp.int32, (part, LANES), 1)
        row = lax.broadcasted_iota(jnp.int32, (part, LANES), 0)
        stores = []
        for k in range(parts):
            at = pl.ds(k * part, part)
            begin = pl.multiple_of((me ^ k) * part, part)
            q = dot_f32(tok[pl.ds(begin, part), :], w[...]) * QUERY_SCALE
            hot = (lane - HD == ((row + begin) >> BLK_BITS)).astype(jnp.float32)
            for p in range(pairs):
                pair = q[:, p * LANES : (p + 1) * LANES]
                held[p, 0, at, :] = jnp.where(lane < HD, pair, hot).astype(jnp.bfloat16)
                held[p, 1, at, :] = jnp.where(lane < HD, swap_halves(pair), hot).astype(jnp.bfloat16)
        for p in range(pairs):
            copy = pltpu.make_async_copy(held.at[p], outs[p], out_sems.at[p])
            copy.start()
            stores.append(copy)
        tables.fill(bias_ref, 0)
        lane = lax.broadcasted_iota(jnp.int32, (rows, LANES), 1)
        for h in range(2):
            peak, total_sum = tables.sweep(
                held[0, h], h, jnp.full((rows, 1), LOWEST, jnp.float32), jnp.zeros((rows, LANES), jnp.float32)
            )
            state_ref[h] = jnp.where(lane == 1, peak, total_sum)
        for copy in stores:
            copy.wait()

    out = pl.pallas_call(
        kernel,
        out_shape=[jax.ShapeDtypeStruct((2, rows, LANES), jnp.bfloat16)] * pairs
        + [jax.ShapeDtypeStruct((sources * 8, LANES), jnp.float32), jax.ShapeDtypeStruct((2, rows, LANES), jnp.float32)],
        in_specs=[VMEM] * 2 + [HBM] * (1 + len(early)),
        out_specs=[ANY] * pairs + [VMEM] * 2,
        scratch_shapes=[
            pltpu.VMEM((pairs, 2, rows, LANES), jnp.bfloat16),
            pltpu.VMEM((LANES, key_blocks), jnp.float32),
            pltpu.VMEM(w_query.shape, jnp.bfloat16),
            pltpu.SemaphoreType.DMA(()),
            pltpu.SemaphoreType.DMA((pairs,)),
        ]
        + table_scratch(early),
        compiler_params=PARAMS,
        cost_estimate=FREE,
        name="begin_attention",
    )(block_mask, tokens, w_query, *early)
    return out[:pairs], out[pairs], out[pairs + 1]


def attend(queries, state, sources, bias, first, parts, begin, count, cost):
    part = queries.shape[1] // parts
    rows = count * part
    states = [] if state is None else [state]

    def kernel(q_ref, bias_ref, *rest):
        state_refs, rest = rest[: len(states)], rest[len(states) :]
        srcs, rest = rest[: len(sources)], rest[len(sources) :]
        outs, scratch = rest[:count], rest[count:]
        tables = Tables(*scratch, srcs)
        tables.fill(bias_ref, first)
        lane = lax.broadcasted_iota(jnp.int32, (rows, LANES), 1)
        low = lane < HD
        taken = slice(begin * part, begin * part + rows)
        sums = []
        for h in range(2):
            if states:
                total_sum = state_refs[0][h, taken]
                peak = jnp.max(jnp.where(lane == 1, total_sum, LOWEST), axis=1, keepdims=True)
                total_sum = jnp.where(lane == 1, pltpu.roll(total_sum, 1, 1), total_sum)
            else:
                peak = jnp.full((rows, 1), LOWEST, jnp.float32)
                total_sum = jnp.zeros((rows, LANES), jnp.float32)
            sums.append(tables.sweep(q_ref[h, taken], h, peak, total_sum)[1])
        top = jnp.where(low, swap_halves(sums[0]), sums[1])
        mass = jnp.where(low, sums[0], swap_halves(sums[1]))
        out = (top / mass).astype(jnp.bfloat16)
        for k in range(count):
            outs[k][...] = out[k * part : (k + 1) * part, :]

    return pl.pallas_call(
        kernel,
        out_shape=[jax.ShapeDtypeStruct((part, LANES), jnp.bfloat16)] * count,
        in_specs=[VMEM, VMEM] + [VMEM] * len(states) + [HBM] * len(sources),
        out_specs=[VMEM] * count,
        scratch_shapes=table_scratch(sources),
        compiler_params=PARAMS,
        cost_estimate=pl.CostEstimate(flops=cost, bytes_accessed=0, transcendentals=0),
        name="attend",
    )(queries, bias, *states, *sources)


def project_out(attended, w_mine, w_other, tiles):
    heads, depth, width = w_mine.shape
    pairs = len(attended[0])
    rows = attended[0][0].shape[0]
    piece = depth // tiles
    order = [0]
    bit = heads // 2
    while bit:
        order += [bit ^ k for k in order]
        bit //= 2
    pieces = [attended[k][p] for k in order for p in range(pairs)]
    direct = depth % LANES == 0

    def kernel(*rest):
        refs, (mine_ref, other_ref, out_ref, *scratch) = rest[: heads * pairs], rest[heads * pairs :]
        quarter = (lax.axis_index("band") & 1) * tiles + lax.axis_index("tiles")
        lane = lax.broadcasted_iota(jnp.int32, (rows, LANES), 1)
        groups = []
        for i in range(heads):
            group = [refs[i * pairs + p][...].astype(jnp.float32) for p in range(pairs)]
            size = piece
            while size < depth * 2:
                flip = (quarter & (size // piece)) > 0
                if size < LANES:
                    moved = [
                        jnp.where((lane & size) > 0, pltpu.roll(x, size, 1), pltpu.roll(x, LANES - size, 1)) for x in group
                    ]
                else:
                    moved = [group[p ^ (size // LANES)] for p in range(pairs)]
                group = [jnp.where(flip, m, x) for m, x in zip(moved, group)]
                size *= 2
            groups.append([x.astype(jnp.bfloat16) for x in group])
        if direct:
            half = depth // LANES
            near_cols = jnp.concatenate([x for group in groups for x in group[:half]], axis=1)
            far_cols = jnp.concatenate([x for group in groups for x in group[half:]], axis=1)
            total = dot_f32(near_cols, mine_ref[...].reshape(heads * depth, width))
            total += dot_f32(far_cols, other_ref[...].reshape(heads * depth, width))
        else:
            w, sems = scratch
            copies = [
                pltpu.make_async_copy(ref, w.at[:, pl.ds(s * depth, depth), :], sems.at[s])
                for s, ref in enumerate((mine_ref, other_ref))
            ]
            for copy in copies:
                copy.start()
            for copy in copies:
                copy.wait()
            cols = jnp.concatenate([x for group in groups for x in group], axis=1)
            total = dot_f32(cols, w[...].reshape(heads * 2 * depth, width))
        out_ref[...] = total.astype(jnp.bfloat16)

    scratch = [] if direct else [pltpu.VMEM((heads, 2 * depth, width), jnp.bfloat16), pltpu.SemaphoreType.DMA((2,))]
    return pl.pallas_call(
        kernel,
        out_shape=jax.ShapeDtypeStruct((rows, width), jnp.bfloat16),
        in_specs=[VMEM] * len(pieces) + [VMEM if direct else ANY] * 2,
        out_specs=VMEM,
        scratch_shapes=scratch,
        compiler_params=SMALL,
        cost_estimate=FREE,
        name="project_out",
    )(*pieces, w_mine, w_other)


def on_device(sizes, tokens, w_query, w_key, w_value, w_out, block_mask):
    tiles, bands, heads = sizes
    hops = range(1, bands // 2)

    def along_band(array, goes_to):
        return lax.ppermute(array, "band", [(i, goes_to(i)) for i in range(bands)])

    def to_sibling(array):
        return along_band(array, lambda i: i ^ 1)

    def along_head(array, k):
        return lax.ppermute(array, "head", [(i, i ^ k) for i in range(heads)])

    def source_bands(band):
        found = [band, band ^ 1]
        for r in hops:
            far = lax.rem(band + bands - 2 * r, bands)
            found += [far, far ^ 1]
        return found

    kv = project_kv(block_mask, tokens, w_key, w_value)
    kv = [list(kv[:2])] + [[one] for one in kv[2:]]
    pairs = len(kv)
    far = [[[along_band(one, lambda i: (i + 2 * r) % bands) for one in arrays] for r in hops] for arrays in kv]
    near = [[to_sibling(one) for one in arrays] for arrays in kv]

    def widen(held, came, k):
        held = jnp.concatenate([held, came]) if came is not None else held
        return held, along_head(held, k)

    def other_tiles(array):
        return [lax.ppermute(array, "tiles", [(i, i ^ s) for i in range(tiles)]) for s in range(1, tiles)]

    quarter = (lax.axis_index("band") & 1) * tiles + lax.axis_index("tiles")
    piece = w_out.shape[0] // (2 * tiles)
    w_mine = lax.dynamic_slice_in_dim(w_out, quarter * piece, piece, 0)
    w_mine, kv = lax.optimization_barrier((w_mine, kv))
    bit = heads // 2
    w_mine, arriving = widen(w_mine[None], None, bit)
    queries, bias, state = begin_attention(block_mask, tokens, w_query, kv[0] + near[0], heads, source_bands)
    far[0], queries, arriving = lax.optimization_barrier((far[0], queries, arriving))
    while bit > 1:
        bit //= 2
        w_mine, arriving = widen(w_mine, arriving, bit)

    attended = [[] for _ in range(heads)]

    def exchange(pieces, first):
        for k, piece in enumerate(pieces, first):
            attended[k].append(piece if k == 0 else along_head(piece, k))

    last = pairs - 1
    if last == 0:
        w_mine = jnp.concatenate([w_mine, arriving])
        arriving = other_tiles(w_mine)
    for p in range(pairs):
        if p > 0:
            far[p], pieces = lax.optimization_barrier((far[p], pieces))
        sources = [] if p == 0 else kv[p] + near[p]
        for arrays in far[p]:
            sources += arrays + [to_sibling(one) for one in arrays]
        held, first = (state, 2) if p == 0 else (None, 0)
        if p < last:
            pieces = attend(queries[p], held, sources, bias, first, heads, 0, heads, 0)
            if p == 0:
                pieces, arriving = lax.optimization_barrier((pieces, arriving))
                w_mine = jnp.concatenate([w_mine, arriving])
                arriving = other_tiles(w_mine)
            exchange(pieces, 0)
        else:
            pieces = attend(queries[p], held, sources, bias, first, heads, 1, heads - 1, 0)
            pieces, attended, sources[-1] = lax.optimization_barrier((pieces, attended, sources[-1]))
            exchange(pieces, 1)
            arriving, sources[-1] = lax.optimization_barrier((arriving, sources[-1]))
            exchange(attend(queries[p], held, sources, bias, first, heads, 0, 1, LONG), 0)
    w_mine = jnp.concatenate([w_mine] + arriving, axis=1)
    return project_out(attended, w_mine, to_sibling(w_mine), tiles)


def solution(mesh):
    sizes = tuple(mesh.shape[axis] for axis in ("tiles", "band", "head"))
    return jax.shard_map(
        functools.partial(on_device, sizes),
        mesh=mesh,
        in_specs=(
            P(("tiles", "band"), None),
            P(None, "head"),
            P(None, "head"),
            P(None, "head"),
            P("head", None),
            P("tiles", None),
        ),
        out_specs=P(("tiles", "band", "head"), None),
        check_vma=False,
    )
```

```python
import functools
import math

import jax
import jax.numpy as jnp
from jax import lax
from jax.experimental import pallas as pl
from jax.experimental.pallas import tpu as pltpu
from jax.sharding import PartitionSpec as P

HD = 64
BLK = 128
KEEP = 6
LANES = 128
NEG = -1e30
LOWEST = -3e38
HELD = KEEP * BLK
CHUNK = 1536
LONG = 2**33
GROUP = 2 * HELD // CHUNK
QUERY_SCALE = HD**-0.5 * math.log2(math.e)
BLK_BITS = 7
BAND_BITS = 3
SMALL = pltpu.CompilerParams(vmem_limit_bytes=16 * 2**20)
FREE = pl.CostEstimate(flops=0, bytes_accessed=0, transcendentals=0)
LARGE = pltpu.CompilerParams(vmem_limit_bytes=60 * 2**20)
PARAMS = pltpu.CompilerParams(vmem_limit_bytes=32 * 2**20)
ANY = pl.BlockSpec(memory_space=pl.ANY)
HBM = pl.BlockSpec(memory_space=pltpu.HBM)
VMEM = pl.BlockSpec(memory_space=pltpu.VMEM)


def dot_f32(left, right):
    return jnp.dot(left, right, preferred_element_type=jnp.float32)


def low_lanes(shape):
    return lax.broadcasted_iota(jnp.int32, shape, len(shape) - 1) < HD


def swap_halves(array):
    return pltpu.roll(array, HD, array.ndim - 1)


def block_ranks(mask):
    blocks = mask.shape[1]
    used = jnp.max(mask.astype(jnp.float32), axis=0, keepdims=True)
    earlier = lax.broadcasted_iota(jnp.int32, (blocks, blocks), 0)
    later = lax.broadcasted_iota(jnp.int32, (blocks, blocks), 1)
    counts = ((earlier >> BAND_BITS) == (later >> BAND_BITS)) & (earlier < later)
    rank = dot_f32(jnp.broadcast_to(used, (8, blocks)).astype(jnp.bfloat16), counts.astype(jnp.float32).astype(jnp.bfloat16))
    return jnp.broadcast_to(used, (8, blocks)), rank


def slots_of(used, rank, band):
    lane = lax.broadcasted_iota(jnp.int32, used.shape, 1)
    slot = lax.broadcasted_iota(jnp.int32, used.shape, 0).astype(jnp.float32)
    return jnp.where(((lane >> BAND_BITS) == band) & (rank == slot), used, 0.0)


def project_kv(block_mask, tokens, w_key, w_value):
    pairs = w_key.shape[1] // LANES
    rows_in = tokens.shape[0]
    rows = KEEP * BLK
    step = 2 * BLK
    steps = tokens.shape[1] // step

    def kernel(mask_any, tok_ref, wk_ref, wv_ref, *rest):
        outs, own_ref, rest = rest[: pairs + 1], rest[pairs + 1], rest[pairs + 2 :]
        (mask_ref, tok, wk, wv, keys, values, held, sems, out_sems) = rest
        load_mask = pltpu.make_async_copy(mask_any, mask_ref, sems.at[0])
        load_mask.start()
        loads = []
        for c in range(steps):
            at = pl.ds(c * step, step)
            loads += [
                pltpu.make_async_copy(wk_ref.at[at, :], wk.at[at, :], sems.at[1 + 3 * c]),
                pltpu.make_async_copy(wv_ref.at[at, :], wv.at[at, :], sems.at[2 + 3 * c]),
                pltpu.make_async_copy(tok_ref.at[:, at], tok.at[:, at], sems.at[3 + 3 * c]),
            ]
        for copy in loads:
            copy.start()
        load_mask.wait()
        used, rank = block_ranks(mask_ref[...])
        picked = slots_of(used, rank, lax.axis_index("band"))
        place = (lax.broadcasted_iota(jnp.int32, picked.shape, 1) & (2**BAND_BITS - 1)).astype(jnp.float32)
        digit = lax.broadcasted_iota(jnp.int32, picked.shape, 0)
        scale = (1 << (BAND_BITS * jnp.minimum(digit, KEEP))).astype(jnp.float32)
        code = jnp.sum(jnp.where(digit < KEEP, picked * place * scale, 0.0)).astype(jnp.int32)
        low = low_lanes((rows_in, LANES))
        for c in range(steps):
            at = pl.ds(c * step, step)
            for copy in loads[3 * c : 3 * c + 3]:
                copy.wait()
            for total, weight in ((keys, wk), (values, wv)):
                product = dot_f32(tok[:, at], weight[at, :])
                if c == 0:
                    total[...] = product
                else:
                    total[...] += product
        for p in range(pairs):
            cols = slice(p * LANES, (p + 1) * LANES)
            k, v = keys[:, cols], values[:, cols]
            held[p, 0] = jnp.where(low, k, swap_halves(v)).astype(jnp.bfloat16)
            held[p, 1] = jnp.where(low, swap_halves(k), v).astype(jnp.bfloat16)
        stores = []
        for p in range(pairs):
            for e in range(KEEP):
                begin = pl.multiple_of(((code >> (BAND_BITS * e)) & (2**BAND_BITS - 1)) * BLK, BLK)
                block, at = pl.ds(begin, BLK), pl.ds(e * BLK, BLK)
                if p == 0:
                    moves = [(held.at[0, h, block, :], outs[h].at[at, :]) for h in range(2)]
                    moves.append((held.at[0, :, block, :], own_ref.at[:, at, :]))
                else:
                    moves = [(held.at[p, :, block, :], outs[p + 1].at[:, at, :])]
                for i, (source, to) in enumerate(moves):
                    copy = pltpu.make_async_copy(source, to, out_sems.at[p, e, i])
                    copy.start()
                    stores.append(copy)
        for copy in stores:
            copy.wait()

    return pl.pallas_call(
        kernel,
        out_shape=[jax.ShapeDtypeStruct((rows, LANES), jnp.bfloat16)] * 2
        + [jax.ShapeDtypeStruct((2, rows, LANES), jnp.bfloat16)] * pairs,
        in_specs=[ANY] * 4,
        out_specs=[ANY] * (pairs + 2),
        scratch_shapes=[
            pltpu.VMEM(block_mask.shape, jnp.int32),
            pltpu.VMEM(tokens.shape, jnp.bfloat16),
            pltpu.VMEM(w_key.shape, jnp.bfloat16),
            pltpu.VMEM(w_value.shape, jnp.bfloat16),
            pltpu.VMEM((rows_in, w_key.shape[1]), jnp.float32),
            pltpu.VMEM((rows_in, w_key.shape[1]), jnp.float32),
            pltpu.VMEM((pairs, 2, rows_in, LANES), jnp.bfloat16),
            pltpu.SemaphoreType.DMA((1 + 3 * steps,)),
            pltpu.SemaphoreType.DMA((pairs, KEEP, 3)),
        ],
        compiler_params=LARGE,
        cost_estimate=FREE,
        name="project_kv",
    )(block_mask, tokens, w_key, w_value)


class Tables:
    def __init__(self, landing, key_tab, value_tab, sems, refs):
        self.landing, self.key_tab, self.value_tab = landing, key_tab, value_tab
        self.copies, taken = [], 0
        for s, ref in enumerate(refs):
            at = pl.ds(taken // 2 * HELD, HELD)
            to = landing.at[taken % 2, at, :] if len(ref.shape) == 2 else landing.at[:, at, :]
            taken += len(ref.shape) - 1
            self.copies.append((taken, pltpu.make_async_copy(ref, to, sems.at[s])))
        for _, copy in self.copies:
            copy.start()

    def fill(self, bias_ref, first):
        low = low_lanes((BLK, LANES)).astype(jnp.float32).astype(jnp.bfloat16)
        high = (1.0 - low_lanes((BLK, LANES)).astype(jnp.float32)).astype(jnp.bfloat16)
        sources = self.landing.shape[1] // HELD
        for s in range(sources):
            for taken, copy in self.copies:
                if 2 * s < taken <= 2 * s + 2:
                    copy.wait()
            for e in range(KEEP):
                at = pl.ds((s * KEEP + e) * BLK, BLK)
                row = (first + s) * 8 + e
                add = jnp.broadcast_to(bias_ref[row : row + 1, :], (BLK, LANES)).astype(jnp.bfloat16)
                for h in range(2):
                    kv = self.landing[h, at, :]
                    self.key_tab[h, at, :] = kv * low + add
                    self.value_tab[h, at, :] = kv * high + low

    def sweep(self, q, h, peak, total_sum):
        def chunk(begin, carried):
            peak, total_sum = carried
            at = pl.ds(begin, CHUNK)
            scores = lax.dot_general(
                q, self.key_tab[h, at, :], (((1,), (1,)), ((), ())), preferred_element_type=jnp.float32
            )
            new_peak = jnp.maximum(peak, jnp.max(scores, axis=1, keepdims=True))
            weights = jnp.exp2(scores - new_peak).astype(jnp.bfloat16)
            total_sum = total_sum * jnp.exp2(peak - new_peak) + dot_f32(weights, self.value_tab[h, at, :])
            return new_peak, total_sum

        def group(g, carried):
            for c in range(GROUP):
                begin = (g * GROUP + c) * CHUNK
                carried = chunk(begin if isinstance(g, int) else pl.multiple_of(begin, CHUNK), carried)
            return carried

        groups = self.key_tab.shape[1] // (GROUP * CHUNK)
        carried = (peak, total_sum)
        if groups > 2:
            return lax.fori_loop(0, groups, group, carried)
        for g in range(groups):
            carried = group(g, carried)
        return carried


def table_scratch(arrays):
    sources = sum(array.ndim - 1 for array in arrays) // 2
    table = pltpu.VMEM((2, sources * HELD, LANES), jnp.bfloat16)
    return [table, table, table, pltpu.SemaphoreType.DMA((len(arrays),))]


def begin_attention(block_mask, tokens, w_query, early, parts, source_bands):
    rows, width = tokens.shape
    pairs = w_query.shape[1] // LANES
    part = rows // parts
    per_band = rows // BLK
    key_blocks = block_mask.shape[1]
    sources = len(source_bands(0))

    def kernel(mask_ref, tok, w_any, *rest):
        early_refs, rest = rest[: len(early)], rest[len(early) :]
        outs = rest[:pairs]
        bias_ref, state_ref, held, own_rows, w, w_sem, out_sems, *scratch = rest[pairs:]
        load_w = pltpu.make_async_copy(w_any, w, w_sem)
        load_w.start()
        tables = Tables(*scratch, early_refs)
        me, band = lax.axis_index("head"), lax.axis_index("band")
        own_rows[...] = jnp.zeros(own_rows.shape, jnp.float32)
        first = pl.multiple_of(band * per_band, per_band)
        own_rows[HD : HD + per_band, :] = mask_ref[pl.ds(first, per_band), :].astype(jnp.float32)
        used, rank = block_ranks(mask_ref[...])
        lane8 = lax.broadcasted_iota(jnp.int32, (8, LANES), 1)
        for s, source in enumerate(source_bands(band)):
            allowed = lax.dot_general(
                slots_of(used, rank, source).astype(jnp.bfloat16),
                own_rows[...].astype(jnp.bfloat16),
                (((1,), (1,)), ((), ())),
                preferred_element_type=jnp.float32,
            )
            queried = (lane8 >= HD) & (lane8 < HD + per_band)
            bias_ref[s * 8 : (s + 1) * 8, :] = jnp.where(queried & (allowed < 0.5), NEG, 0.0)
        load_w.wait()
        lane = lax.broadcasted_iota(jnp.int32, (part, LANES), 1)
        row = lax.broadcasted_iota(jnp.int32, (part, LANES), 0)
        stores = []
        for k in range(parts):
            at = pl.ds(k * part, part)
            begin = pl.multiple_of((me ^ k) * part, part)
            q = dot_f32(tok[pl.ds(begin, part), :], w[...]) * QUERY_SCALE
            hot = (lane - HD == ((row + begin) >> BLK_BITS)).astype(jnp.float32)
            for p in range(pairs):
                pair = q[:, p * LANES : (p + 1) * LANES]
                held[p, 0, at, :] = jnp.where(lane < HD, pair, hot).astype(jnp.bfloat16)
                held[p, 1, at, :] = jnp.where(lane < HD, swap_halves(pair), hot).astype(jnp.bfloat16)
        for p in range(pairs):
            copy = pltpu.make_async_copy(held.at[p], outs[p], out_sems.at[p])
            copy.start()
            stores.append(copy)
        tables.fill(bias_ref, 0)
        lane = lax.broadcasted_iota(jnp.int32, (rows, LANES), 1)
        for h in range(2):
            peak, total_sum = tables.sweep(
                held[0, h], h, jnp.full((rows, 1), LOWEST, jnp.float32), jnp.zeros((rows, LANES), jnp.float32)
            )
            state_ref[h] = jnp.where(lane == 1, peak, total_sum)
        for copy in stores:
            copy.wait()

    out = pl.pallas_call(
        kernel,
        out_shape=[jax.ShapeDtypeStruct((2, rows, LANES), jnp.bfloat16)] * pairs
        + [jax.ShapeDtypeStruct((sources * 8, LANES), jnp.float32), jax.ShapeDtypeStruct((2, rows, LANES), jnp.float32)],
        in_specs=[VMEM] * 2 + [HBM] * (1 + len(early)),
        out_specs=[ANY] * pairs + [VMEM] * 2,
        scratch_shapes=[
            pltpu.VMEM((pairs, 2, rows, LANES), jnp.bfloat16),
            pltpu.VMEM((LANES, key_blocks), jnp.float32),
            pltpu.VMEM(w_query.shape, jnp.bfloat16),
            pltpu.SemaphoreType.DMA(()),
            pltpu.SemaphoreType.DMA((pairs,)),
        ]
        + table_scratch(early),
        compiler_params=PARAMS,
        cost_estimate=FREE,
        name="begin_attention",
    )(block_mask, tokens, w_query, *early)
    return out[:pairs], out[pairs], out[pairs + 1]


def attend(queries, state, sources, bias, first, parts, begin, count, cost):
    part = queries.shape[1] // parts
    rows = count * part
    states = [] if state is None else [state]

    def kernel(q_ref, bias_ref, *rest):
        state_refs, rest = rest[: len(states)], rest[len(states) :]
        srcs, rest = rest[: len(sources)], rest[len(sources) :]
        outs, scratch = rest[:count], rest[count:]
        tables = Tables(*scratch, srcs)
        tables.fill(bias_ref, first)
        lane = lax.broadcasted_iota(jnp.int32, (rows, LANES), 1)
        low = lane < HD
        taken = slice(begin * part, begin * part + rows)
        sums = []
        for h in range(2):
            if states:
                total_sum = state_refs[0][h, taken]
                peak = jnp.max(jnp.where(lane == 1, total_sum, LOWEST), axis=1, keepdims=True)
                total_sum = jnp.where(lane == 1, pltpu.roll(total_sum, 1, 1), total_sum)
            else:
                peak = jnp.full((rows, 1), LOWEST, jnp.float32)
                total_sum = jnp.zeros((rows, LANES), jnp.float32)
            sums.append(tables.sweep(q_ref[h, taken], h, peak, total_sum)[1])
        top = jnp.where(low, swap_halves(sums[0]), sums[1])
        mass = jnp.where(low, sums[0], swap_halves(sums[1]))
        out = (top / mass).astype(jnp.bfloat16)
        for k in range(count):
            outs[k][...] = out[k * part : (k + 1) * part, :]

    return pl.pallas_call(
        kernel,
        out_shape=[jax.ShapeDtypeStruct((part, LANES), jnp.bfloat16)] * count,
        in_specs=[VMEM, VMEM] + [VMEM] * len(states) + [HBM] * len(sources),
        out_specs=[VMEM] * count,
        scratch_shapes=table_scratch(sources),
        compiler_params=PARAMS,
        cost_estimate=pl.CostEstimate(flops=cost, bytes_accessed=0, transcendentals=0),
        name="attend",
    )(queries, bias, *states, *sources)


def project_out(attended, w_out, w_mine, w_other, tiles):
    depth, width = w_mine.shape[1:]
    heads, pairs = len(attended), len(attended[0])
    rows = attended[0][0].shape[0]
    piece = depth // tiles
    order = [0]
    bit = heads // 2
    while bit:
        order += [bit ^ k for k in order]
        bit //= 2
    pieces = [attended[k][p] for k in order for p in range(pairs)]
    direct = depth % LANES == 0

    def kernel(*rest):
        refs, (own_ref, mine_ref, other_ref, out_ref, *scratch) = rest[: heads * pairs], rest[heads * pairs :]
        if not direct:
            w, sems = scratch
            copies = [
                pltpu.make_async_copy(ref, w.at[:, pl.ds(s * depth, depth), :], sems.at[s])
                for s, ref in enumerate((mine_ref, other_ref))
            ]
            for copy in copies:
                copy.start()
        quarter = (lax.axis_index("band") & 1) * tiles + lax.axis_index("tiles")
        lane = lax.broadcasted_iota(jnp.int32, (rows, LANES), 1)
        groups = []
        for i in range(1, heads):
            group = [refs[i * pairs + p][...].astype(jnp.float32) for p in range(pairs)]
            size = piece
            while size < depth * 2:
                flip = (quarter & (size // piece)) > 0
                if size < LANES:
                    moved = [
                        jnp.where((lane & size) > 0, pltpu.roll(x, size, 1), pltpu.roll(x, LANES - size, 1)) for x in group
                    ]
                else:
                    moved = [group[p ^ (size // LANES)] for p in range(pairs)]
                group = [jnp.where(flip, m, x) for m, x in zip(moved, group)]
                size *= 2
            groups.append([x.astype(jnp.bfloat16) for x in group])
        total = dot_f32(jnp.concatenate([ref[...] for ref in refs[:pairs]], axis=1), own_ref[...])
        if direct:
            half = depth // LANES
            near_cols = jnp.concatenate([x for group in groups for x in group[:half]], axis=1)
            far_cols = jnp.concatenate([x for group in groups for x in group[half:]], axis=1)
            total += dot_f32(near_cols, mine_ref[...].reshape((heads - 1) * depth, width))
            total += dot_f32(far_cols, other_ref[...].reshape((heads - 1) * depth, width))
        else:
            for copy in copies:
                copy.wait()
            cols = jnp.concatenate([x for group in groups for x in group], axis=1)
            total += dot_f32(cols, w[...].reshape((heads - 1) * 2 * depth, width))
        out_ref[...] = total.astype(jnp.bfloat16)

    scratch = [pltpu.VMEM((heads - 1, 2 * depth, width), jnp.bfloat16), pltpu.SemaphoreType.DMA((2,))]
    return pl.pallas_call(
        kernel,
        out_shape=jax.ShapeDtypeStruct((rows, width), jnp.bfloat16),
        in_specs=[VMEM] * (len(pieces) + 1) + [VMEM if direct else ANY] * 2,
        out_specs=VMEM,
        scratch_shapes=[] if direct else scratch,
        compiler_params=SMALL,
        cost_estimate=FREE,
        name="project_out",
    )(*pieces, w_out, w_mine, w_other)


def on_device(sizes, tokens, w_query, w_key, w_value, w_out, block_mask):
    tiles, bands, heads = sizes
    hops = range(1, bands // 2)

    def along_band(array, goes_to):
        return lax.ppermute(array, "band", [(i, goes_to(i)) for i in range(bands)])

    def to_sibling(array):
        return along_band(array, lambda i: i ^ 1)

    def along_head(array, k):
        return lax.ppermute(array, "head", [(i, i ^ k) for i in range(heads)])

    def source_bands(band):
        found = [band, band ^ 1]
        for r in hops:
            far = lax.rem(band + bands - 2 * r, bands)
            found += [far, far ^ 1]
        return found

    kv = project_kv(block_mask, tokens, w_key, w_value)
    *kv, own = kv
    kv = [list(kv[:2])] + [[one] for one in kv[2:]]
    pairs = len(kv)
    far = [[[along_band(one, lambda i: (i + 2 * r) % bands) for one in arrays] for r in hops] for arrays in kv]
    near = [[to_sibling(one) for one in arrays] for arrays in kv]

    def widen(held, came, k):
        held = jnp.concatenate([held, came]) if came is not None else held
        return held, along_head(held, k)

    def other_tiles(array):
        return [lax.ppermute(array, "tiles", [(i, i ^ s) for i in range(tiles)]) for s in range(1, tiles)]

    quarter = (lax.axis_index("band") & 1) * tiles + lax.axis_index("tiles")
    piece = w_out.shape[0] // (2 * tiles)
    w_mine = lax.dynamic_slice_in_dim(w_out, quarter * piece, piece, 0)
    w_mine, kv = lax.optimization_barrier((w_mine, kv))
    bit = heads // 2
    w_mine, arriving = widen(w_mine[None], None, bit)
    queries, bias, state = begin_attention(block_mask, tokens, w_query, [own] + near[0], heads, source_bands)
    far[0], queries, arriving = lax.optimization_barrier((far[0], queries, arriving))
    while bit > 1:
        bit //= 2
        w_mine, arriving = widen(w_mine, arriving, bit)

    attended = [[] for _ in range(heads)]

    def exchange(pieces, first):
        for k, piece in enumerate(pieces, first):
            attended[k].append(piece if k == 0 else along_head(piece, k))

    last = pairs - 1
    if last == 0:
        w_mine = jnp.concatenate([w_mine, arriving])[1:]
        arriving = other_tiles(w_mine)
    for p in range(pairs):
        if p > 0:
            far[p], pieces = lax.optimization_barrier((far[p], pieces))
        sources = [] if p == 0 else kv[p] + near[p]
        for arrays in far[p]:
            sources += arrays + [to_sibling(one) for one in arrays]
        held, first = (state, 2) if p == 0 else (None, 0)
        if p < last:
            pieces = attend(queries[p], held, sources, bias, first, heads, 0, heads, 0)
            if p == 0:
                pieces, arriving = lax.optimization_barrier((pieces, arriving))
                w_mine = jnp.concatenate([w_mine, arriving])[1:]
                arriving = other_tiles(w_mine)
            exchange(pieces, 0)
        else:
            pieces = attend(queries[p], held, sources, bias, first, heads, 1, heads - 1, 2**31)
            pieces, attended, sources[-1] = lax.optimization_barrier((pieces, attended, sources[-1]))
            exchange(pieces, 1)
            arriving, sources[-1] = lax.optimization_barrier((arriving, sources[-1]))
            exchange(attend(queries[p], held, sources, bias, first, heads, 0, 1, LONG), 0)
    w_mine = jnp.concatenate([w_mine] + arriving, axis=1)
    return project_out(attended, w_out, w_mine, to_sibling(w_mine), tiles)


def solution(mesh):
    sizes = tuple(mesh.shape[axis] for axis in ("tiles", "band", "head"))
    return jax.shard_map(
        functools.partial(on_device, sizes),
        mesh=mesh,
        in_specs=(
            P(("tiles", "band"), None),
            P(None, "head"),
            P(None, "head"),
            P(None, "head"),
            P("head", None),
            P("tiles", None),
        ),
        out_specs=P(("tiles", "band", "head"), None),
        check_vma=False,
    )
```

```python
import functools
import math

import jax
import jax.numpy as jnp
from jax import lax
from jax.experimental import pallas as pl
from jax.experimental.pallas import tpu as pltpu
from jax.sharding import PartitionSpec as P

HD = 64
BLK = 128
KEEP = 6
LANES = 128
NEG = -1e30
LOWEST = -3e38
HELD = KEEP * BLK
CHUNK = 1536
LONG = 2**33
GROUP = 2 * HELD // CHUNK
QUERY_SCALE = HD**-0.5 * math.log2(math.e)
BLK_BITS = 7
BAND_BITS = 3
SMALL = pltpu.CompilerParams(vmem_limit_bytes=16 * 2**20)
FREE = pl.CostEstimate(flops=0, bytes_accessed=0, transcendentals=0)
LARGE = pltpu.CompilerParams(vmem_limit_bytes=60 * 2**20)
PARAMS = pltpu.CompilerParams(vmem_limit_bytes=32 * 2**20)
ANY = pl.BlockSpec(memory_space=pl.ANY)
HBM = pl.BlockSpec(memory_space=pltpu.HBM)
VMEM = pl.BlockSpec(memory_space=pltpu.VMEM)


def dot_f32(left, right):
    return jnp.dot(left, right, preferred_element_type=jnp.float32)


def low_lanes(shape):
    return lax.broadcasted_iota(jnp.int32, shape, len(shape) - 1) < HD


def swap_halves(array):
    return pltpu.roll(array, HD, array.ndim - 1)


def block_ranks(mask):
    blocks = mask.shape[1]
    used = jnp.max(mask.astype(jnp.float32), axis=0, keepdims=True)
    earlier = lax.broadcasted_iota(jnp.int32, (blocks, blocks), 0)
    later = lax.broadcasted_iota(jnp.int32, (blocks, blocks), 1)
    counts = ((earlier >> BAND_BITS) == (later >> BAND_BITS)) & (earlier < later)
    rank = dot_f32(jnp.broadcast_to(used, (8, blocks)).astype(jnp.bfloat16), counts.astype(jnp.float32).astype(jnp.bfloat16))
    return jnp.broadcast_to(used, (8, blocks)), rank


def slots_of(used, rank, band):
    lane = lax.broadcasted_iota(jnp.int32, used.shape, 1)
    slot = lax.broadcasted_iota(jnp.int32, used.shape, 0).astype(jnp.float32)
    return jnp.where(((lane >> BAND_BITS) == band) & (rank == slot), used, 0.0)


def project_kv(block_mask, tokens, w_key, w_value):
    pairs = w_key.shape[1] // LANES
    rows = KEEP * BLK
    step = 2 * BLK
    steps = tokens.shape[1] // step

    def kernel(mask_any, tok_ref, wk_ref, wv_ref, *rest):
        outs, own_ref, rest = rest[: pairs + 1], rest[pairs + 1], rest[pairs + 2 :]
        (mask_ref, tok, wk, wv, keys, values, held, sems, out_sems) = rest
        load_mask = pltpu.make_async_copy(mask_any, mask_ref, sems.at[0])
        load_mask.start()
        loads = []
        for c in range(steps):
            at = pl.ds(c * step, step)
            loads += [
                pltpu.make_async_copy(wk_ref.at[at, :], wk.at[at, :], sems.at[1 + 3 * c]),
                pltpu.make_async_copy(wv_ref.at[at, :], wv.at[at, :], sems.at[2 + 3 * c]),
                pltpu.make_async_copy(tok_ref.at[:, at], tok.at[:, at], sems.at[3 + 3 * c]),
            ]
        for copy in loads:
            copy.start()
        load_mask.wait()
        used, rank = block_ranks(mask_ref[...])
        picked = slots_of(used, rank, lax.axis_index("band"))
        place = (lax.broadcasted_iota(jnp.int32, picked.shape, 1) & (2**BAND_BITS - 1)).astype(jnp.float32)
        digit = lax.broadcasted_iota(jnp.int32, picked.shape, 0)
        scale = (1 << (BAND_BITS * jnp.minimum(digit, KEEP))).astype(jnp.float32)
        code = jnp.sum(jnp.where(digit < KEEP, picked * place * scale, 0.0)).astype(jnp.int32)
        low = low_lanes((rows, LANES))
        begins = [pl.multiple_of(((code >> (BAND_BITS * e)) & (2**BAND_BITS - 1)) * BLK, BLK) for e in range(KEEP)]
        for c in range(steps):
            at = pl.ds(c * step, step)
            for copy in loads[3 * c : 3 * c + 3]:
                copy.wait()
            chosen = jnp.concatenate([tok[pl.ds(begin, BLK), at] for begin in begins], axis=0)
            for total, weight in ((keys, wk), (values, wv)):
                product = dot_f32(chosen, weight[at, :])
                if c == 0:
                    total[...] = product
                else:
                    total[...] += product
        for p in range(pairs):
            cols = slice(p * LANES, (p + 1) * LANES)
            k, v = keys[:, cols], values[:, cols]
            held[p, 0] = jnp.where(low, k, swap_halves(v)).astype(jnp.bfloat16)
            held[p, 1] = jnp.where(low, swap_halves(k), v).astype(jnp.bfloat16)
        moves = [(held.at[0, 0], outs[0]), (held.at[0, 1], outs[1]), (held.at[0], own_ref)]
        moves += [(held.at[p], outs[p + 1]) for p in range(1, pairs)]
        stores = [pltpu.make_async_copy(source, to, out_sems.at[i]) for i, (source, to) in enumerate(moves)]
        for copy in stores:
            copy.start()
        for copy in stores:
            copy.wait()

    return pl.pallas_call(
        kernel,
        out_shape=[jax.ShapeDtypeStruct((rows, LANES), jnp.bfloat16)] * 2
        + [jax.ShapeDtypeStruct((2, rows, LANES), jnp.bfloat16)] * pairs,
        in_specs=[ANY] * 4,
        out_specs=[ANY] * (pairs + 2),
        scratch_shapes=[
            pltpu.VMEM(block_mask.shape, jnp.int32),
            pltpu.VMEM(tokens.shape, jnp.bfloat16),
            pltpu.VMEM(w_key.shape, jnp.bfloat16),
            pltpu.VMEM(w_value.shape, jnp.bfloat16),
            pltpu.VMEM((rows, w_key.shape[1]), jnp.float32),
            pltpu.VMEM((rows, w_key.shape[1]), jnp.float32),
            pltpu.VMEM((pairs, 2, rows, LANES), jnp.bfloat16),
            pltpu.SemaphoreType.DMA((1 + 3 * steps,)),
            pltpu.SemaphoreType.DMA((pairs + 2,)),
        ],
        compiler_params=LARGE,
        cost_estimate=FREE,
        name="project_kv",
    )(block_mask, tokens, w_key, w_value)


class Tables:
    def __init__(self, landing, key_tab, value_tab, sems, refs):
        self.landing, self.key_tab, self.value_tab = landing, key_tab, value_tab
        self.copies, taken = [], 0
        for s, ref in enumerate(refs):
            at = pl.ds(taken // 2 * HELD, HELD)
            to = landing.at[taken % 2, at, :] if len(ref.shape) == 2 else landing.at[:, at, :]
            taken += len(ref.shape) - 1
            self.copies.append((taken, pltpu.make_async_copy(ref, to, sems.at[s])))
        for _, copy in self.copies:
            copy.start()

    def fill(self, bias_ref, first):
        low = low_lanes((BLK, LANES)).astype(jnp.float32).astype(jnp.bfloat16)
        high = (1.0 - low_lanes((BLK, LANES)).astype(jnp.float32)).astype(jnp.bfloat16)
        sources = self.landing.shape[1] // HELD
        for s in range(sources):
            for taken, copy in self.copies:
                if 2 * s < taken <= 2 * s + 2:
                    copy.wait()
            for e in range(KEEP):
                at = pl.ds((s * KEEP + e) * BLK, BLK)
                row = (first + s) * 8 + e
                add = jnp.broadcast_to(bias_ref[row : row + 1, :], (BLK, LANES)).astype(jnp.bfloat16)
                for h in range(2):
                    kv = self.landing[h, at, :]
                    self.key_tab[h, at, :] = kv * low + add
                    self.value_tab[h, at, :] = kv * high + low

    def sweep(self, q, h, peak, total_sum):
        def chunk(begin, carried):
            peak, total_sum = carried
            at = pl.ds(begin, CHUNK)
            scores = lax.dot_general(
                q, self.key_tab[h, at, :], (((1,), (1,)), ((), ())), preferred_element_type=jnp.float32
            )
            new_peak = jnp.maximum(peak, jnp.max(scores, axis=1, keepdims=True))
            weights = jnp.exp2(scores - new_peak).astype(jnp.bfloat16)
            total_sum = total_sum * jnp.exp2(peak - new_peak) + dot_f32(weights, self.value_tab[h, at, :])
            return new_peak, total_sum

        def group(g, carried):
            for c in range(GROUP):
                begin = (g * GROUP + c) * CHUNK
                carried = chunk(begin if isinstance(g, int) else pl.multiple_of(begin, CHUNK), carried)
            return carried

        groups = self.key_tab.shape[1] // (GROUP * CHUNK)
        carried = (peak, total_sum)
        if groups > 2:
            return lax.fori_loop(0, groups, group, carried)
        for g in range(groups):
            carried = group(g, carried)
        return carried


def table_scratch(arrays):
    sources = sum(array.ndim - 1 for array in arrays) // 2
    table = pltpu.VMEM((2, sources * HELD, LANES), jnp.bfloat16)
    return [table, table, table, pltpu.SemaphoreType.DMA((len(arrays),))]


def begin_attention(block_mask, tokens, w_query, early, parts, source_bands):
    rows, width = tokens.shape
    pairs = w_query.shape[1] // LANES
    part = rows // parts
    per_band = rows // BLK
    key_blocks = block_mask.shape[1]
    sources = len(source_bands(0))

    def kernel(mask_ref, tok, w_any, *rest):
        early_refs, rest = rest[: len(early)], rest[len(early) :]
        outs = rest[:pairs]
        bias_ref, state_ref, held, own_rows, w, w_sem, out_sems, *scratch = rest[pairs:]
        load_w = pltpu.make_async_copy(w_any, w, w_sem)
        load_w.start()
        tables = Tables(*scratch, early_refs)
        me, band = lax.axis_index("head"), lax.axis_index("band")
        own_rows[...] = jnp.zeros(own_rows.shape, jnp.float32)
        first = pl.multiple_of(band * per_band, per_band)
        own_rows[HD : HD + per_band, :] = mask_ref[pl.ds(first, per_band), :].astype(jnp.float32)
        used, rank = block_ranks(mask_ref[...])
        lane8 = lax.broadcasted_iota(jnp.int32, (8, LANES), 1)
        for s, source in enumerate(source_bands(band)):
            allowed = lax.dot_general(
                slots_of(used, rank, source).astype(jnp.bfloat16),
                own_rows[...].astype(jnp.bfloat16),
                (((1,), (1,)), ((), ())),
                preferred_element_type=jnp.float32,
            )
            queried = (lane8 >= HD) & (lane8 < HD + per_band)
            bias_ref[s * 8 : (s + 1) * 8, :] = jnp.where(queried & (allowed < 0.5), NEG, 0.0)
        load_w.wait()
        lane = lax.broadcasted_iota(jnp.int32, (part, LANES), 1)
        row = lax.broadcasted_iota(jnp.int32, (part, LANES), 0)
        stores = []
        for k in range(parts):
            at = pl.ds(k * part, part)
            begin = pl.multiple_of((me ^ k) * part, part)
            q = dot_f32(tok[pl.ds(begin, part), :], w[...]) * QUERY_SCALE
            hot = (lane - HD == ((row + begin) >> BLK_BITS)).astype(jnp.float32)
            for p in range(pairs):
                pair = q[:, p * LANES : (p + 1) * LANES]
                held[p, 0, at, :] = jnp.where(lane < HD, pair, hot).astype(jnp.bfloat16)
                held[p, 1, at, :] = jnp.where(lane < HD, swap_halves(pair), hot).astype(jnp.bfloat16)
        for p in range(pairs):
            copy = pltpu.make_async_copy(held.at[p], outs[p], out_sems.at[p])
            copy.start()
            stores.append(copy)
        tables.fill(bias_ref, 0)
        lane = lax.broadcasted_iota(jnp.int32, (rows, LANES), 1)
        for h in range(2):
            peak, total_sum = tables.sweep(
                held[0, h], h, jnp.full((rows, 1), LOWEST, jnp.float32), jnp.zeros((rows, LANES), jnp.float32)
            )
            state_ref[h] = jnp.where(lane == 1, peak, total_sum)
        for copy in stores:
            copy.wait()

    out = pl.pallas_call(
        kernel,
        out_shape=[jax.ShapeDtypeStruct((2, rows, LANES), jnp.bfloat16)] * pairs
        + [jax.ShapeDtypeStruct((sources * 8, LANES), jnp.float32), jax.ShapeDtypeStruct((2, rows, LANES), jnp.float32)],
        in_specs=[VMEM] * 2 + [HBM] * (1 + len(early)),
        out_specs=[ANY] * pairs + [VMEM] * 2,
        scratch_shapes=[
            pltpu.VMEM((pairs, 2, rows, LANES), jnp.bfloat16),
            pltpu.VMEM((LANES, key_blocks), jnp.float32),
            pltpu.VMEM(w_query.shape, jnp.bfloat16),
            pltpu.SemaphoreType.DMA(()),
            pltpu.SemaphoreType.DMA((pairs,)),
        ]
        + table_scratch(early),
        compiler_params=PARAMS,
        cost_estimate=FREE,
        name="begin_attention",
    )(block_mask, tokens, w_query, *early)
    return out[:pairs], out[pairs], out[pairs + 1]


def attend(queries, state, sources, bias, first, parts, begin, count, cost):
    part = queries.shape[1] // parts
    rows = count * part
    states = [] if state is None else [state]

    def kernel(q_ref, bias_ref, *rest):
        state_refs, rest = rest[: len(states)], rest[len(states) :]
        srcs, rest = rest[: len(sources)], rest[len(sources) :]
        outs, scratch = rest[:count], rest[count:]
        tables = Tables(*scratch, srcs)
        tables.fill(bias_ref, first)
        lane = lax.broadcasted_iota(jnp.int32, (rows, LANES), 1)
        low = lane < HD
        taken = slice(begin * part, begin * part + rows)
        sums = []
        for h in range(2):
            if states:
                total_sum = state_refs[0][h, taken]
                peak = jnp.max(jnp.where(lane == 1, total_sum, LOWEST), axis=1, keepdims=True)
                total_sum = jnp.where(lane == 1, pltpu.roll(total_sum, 1, 1), total_sum)
            else:
                peak = jnp.full((rows, 1), LOWEST, jnp.float32)
                total_sum = jnp.zeros((rows, LANES), jnp.float32)
            sums.append(tables.sweep(q_ref[h, taken], h, peak, total_sum)[1])
        top = jnp.where(low, swap_halves(sums[0]), sums[1])
        mass = jnp.where(low, sums[0], swap_halves(sums[1]))
        out = (top / mass).astype(jnp.bfloat16)
        for k in range(count):
            outs[k][...] = out[k * part : (k + 1) * part, :]

    return pl.pallas_call(
        kernel,
        out_shape=[jax.ShapeDtypeStruct((part, LANES), jnp.bfloat16)] * count,
        in_specs=[VMEM, VMEM] + [VMEM] * len(states) + [HBM] * len(sources),
        out_specs=[VMEM] * count,
        scratch_shapes=table_scratch(sources),
        compiler_params=PARAMS,
        cost_estimate=pl.CostEstimate(flops=cost, bytes_accessed=0, transcendentals=0),
        name="attend",
    )(queries, bias, *states, *sources)


def project_out(attended, w_out, w_mine, w_other, tiles):
    depth, width = w_mine.shape[1:]
    heads, pairs = len(attended), len(attended[0])
    rows = attended[0][0].shape[0]
    piece = depth // tiles
    order = [0]
    bit = heads // 2
    while bit:
        order += [bit ^ k for k in order]
        bit //= 2
    pieces = [attended[k][p] for k in order for p in range(pairs)]
    direct = depth % LANES == 0

    def kernel(*rest):
        refs, (own_ref, mine_ref, other_ref, out_ref, *scratch) = rest[: heads * pairs], rest[heads * pairs :]
        if not direct:
            w, sems = scratch
            copies = [
                pltpu.make_async_copy(ref, w.at[:, pl.ds(s * depth, depth), :], sems.at[s])
                for s, ref in enumerate((mine_ref, other_ref))
            ]
            for copy in copies:
                copy.start()
        quarter = (lax.axis_index("band") & 1) * tiles + lax.axis_index("tiles")
        lane = lax.broadcasted_iota(jnp.int32, (rows, LANES), 1)
        groups = []
        for i in range(1, heads):
            group = [refs[i * pairs + p][...].astype(jnp.float32) for p in range(pairs)]
            size = piece
            while size < depth * 2:
                flip = (quarter & (size // piece)) > 0
                if size < LANES:
                    moved = [
                        jnp.where((lane & size) > 0, pltpu.roll(x, size, 1), pltpu.roll(x, LANES - size, 1)) for x in group
                    ]
                else:
                    moved = [group[p ^ (size // LANES)] for p in range(pairs)]
                group = [jnp.where(flip, m, x) for m, x in zip(moved, group)]
                size *= 2
            groups.append([x.astype(jnp.bfloat16) for x in group])
        total = dot_f32(jnp.concatenate([ref[...] for ref in refs[:pairs]], axis=1), own_ref[...])
        if direct:
            half = depth // LANES
            near_cols = jnp.concatenate([x for group in groups for x in group[:half]], axis=1)
            far_cols = jnp.concatenate([x for group in groups for x in group[half:]], axis=1)
            total += dot_f32(near_cols, mine_ref[...].reshape((heads - 1) * depth, width))
            total += dot_f32(far_cols, other_ref[...].reshape((heads - 1) * depth, width))
        else:
            for copy in copies:
                copy.wait()
            cols = jnp.concatenate([x for group in groups for x in group], axis=1)
            total += dot_f32(cols, w[...].reshape((heads - 1) * 2 * depth, width))
        out_ref[...] = total.astype(jnp.bfloat16)

    scratch = [pltpu.VMEM((heads - 1, 2 * depth, width), jnp.bfloat16), pltpu.SemaphoreType.DMA((2,))]
    return pl.pallas_call(
        kernel,
        out_shape=jax.ShapeDtypeStruct((rows, width), jnp.bfloat16),
        in_specs=[VMEM] * (len(pieces) + 1) + [VMEM if direct else ANY] * 2,
        out_specs=VMEM,
        scratch_shapes=[] if direct else scratch,
        compiler_params=SMALL,
        cost_estimate=FREE,
        name="project_out",
    )(*pieces, w_out, w_mine, w_other)


def on_device(sizes, tokens, w_query, w_key, w_value, w_out, block_mask):
    tiles, bands, heads = sizes
    hops = range(1, bands // 2)

    def along_band(array, goes_to):
        return lax.ppermute(array, "band", [(i, goes_to(i)) for i in range(bands)])

    def to_sibling(array):
        return along_band(array, lambda i: i ^ 1)

    def along_head(array, k):
        return lax.ppermute(array, "head", [(i, i ^ k) for i in range(heads)])

    def source_bands(band):
        found = [band, band ^ 1]
        for r in hops:
            far = lax.rem(band + bands - 2 * r, bands)
            found += [far, far ^ 1]
        return found

    kv = project_kv(block_mask, tokens, w_key, w_value)
    *kv, own = kv
    kv = [list(kv[:2])] + [[one] for one in kv[2:]]
    pairs = len(kv)
    far = [[[along_band(one, lambda i: (i + 2 * r) % bands) for one in arrays] for r in hops] for arrays in kv]
    near = [[to_sibling(one) for one in arrays] for arrays in kv]

    def widen(held, came, k):
        held = jnp.concatenate([held, came]) if came is not None else held
        return held, along_head(held, k)

    def other_tiles(array):
        return [lax.ppermute(array, "tiles", [(i, i ^ s) for i in range(tiles)]) for s in range(1, tiles)]

    quarter = (lax.axis_index("band") & 1) * tiles + lax.axis_index("tiles")
    piece = w_out.shape[0] // (2 * tiles)
    w_mine = lax.dynamic_slice_in_dim(w_out, quarter * piece, piece, 0)
    w_mine, kv = lax.optimization_barrier((w_mine, kv))
    bit = heads // 2
    w_mine, arriving = widen(w_mine[None], None, bit)
    queries, bias, state = begin_attention(block_mask, tokens, w_query, [own] + near[0], heads, source_bands)
    far[0], queries, arriving = lax.optimization_barrier((far[0], queries, arriving))
    while bit > 1:
        bit //= 2
        w_mine, arriving = widen(w_mine, arriving, bit)

    attended = [[] for _ in range(heads)]

    def exchange(pieces, first):
        for k, piece in enumerate(pieces, first):
            attended[k].append(piece if k == 0 else along_head(piece, k))

    last = pairs - 1
    if last == 0:
        w_mine = jnp.concatenate([w_mine, arriving])[1:]
        arriving = other_tiles(w_mine)
    for p in range(pairs):
        if p > 0:
            far[p], pieces = lax.optimization_barrier((far[p], pieces))
        sources = [] if p == 0 else kv[p] + near[p]
        for arrays in far[p]:
            sources += arrays + [to_sibling(one) for one in arrays]
        held, first = (state, 2) if p == 0 else (None, 0)
        if p < last:
            pieces = attend(queries[p], held, sources, bias, first, heads, 0, heads, 0)
            if p == 0:
                pieces, arriving = lax.optimization_barrier((pieces, arriving))
                w_mine = jnp.concatenate([w_mine, arriving])[1:]
                arriving = other_tiles(w_mine)
            exchange(pieces, 0)
        else:
            pieces = attend(queries[p], held, sources, bias, first, heads, 1, heads - 1, 2**31)
            pieces, attended, sources[-1] = lax.optimization_barrier((pieces, attended, sources[-1]))
            exchange(pieces, 1)
            arriving, sources[-1] = lax.optimization_barrier((arriving, sources[-1]))
            exchange(attend(queries[p], held, sources, bias, first, heads, 0, 1, LONG), 0)
    w_mine = jnp.concatenate([w_mine] + arriving, axis=1)
    return project_out(attended, w_out, w_mine, to_sibling(w_mine), tiles)


def solution(mesh):
    sizes = tuple(mesh.shape[axis] for axis in ("tiles", "band", "head"))
    return jax.shard_map(
        functools.partial(on_device, sizes),
        mesh=mesh,
        in_specs=(
            P(("tiles", "band"), None),
            P(None, "head"),
            P(None, "head"),
            P(None, "head"),
            P("head", None),
            P("tiles", None),
        ),
        out_specs=P(("tiles", "band", "head"), None),
        check_vma=False,
    )
```

```python
import functools
import math

import jax
import jax.numpy as jnp
from jax import lax
from jax.experimental import pallas as pl
from jax.experimental.pallas import tpu as pltpu
from jax.sharding import PartitionSpec as P

HD = 64
BLK = 128
KEEP = 6
LANES = 128
NEG = -1e30
LOWEST = -3e38
HELD = KEEP * BLK
CHUNK = 1536
LONG = 2**33
GROUP = 2 * HELD // CHUNK
QUERY_SCALE = HD**-0.5 * math.log2(math.e)
BLK_BITS = 7
BAND_BITS = 3
SMALL = pltpu.CompilerParams(vmem_limit_bytes=16 * 2**20)
FREE = pl.CostEstimate(flops=0, bytes_accessed=0, transcendentals=0)
LARGE = pltpu.CompilerParams(vmem_limit_bytes=60 * 2**20)
PARAMS = pltpu.CompilerParams(vmem_limit_bytes=32 * 2**20)
ANY = pl.BlockSpec(memory_space=pl.ANY)
HBM = pl.BlockSpec(memory_space=pltpu.HBM)
VMEM = pl.BlockSpec(memory_space=pltpu.VMEM)


def dot_f32(left, right):
    return jnp.dot(left, right, preferred_element_type=jnp.float32)


def low_lanes(shape):
    return lax.broadcasted_iota(jnp.int32, shape, len(shape) - 1) < HD


def swap_halves(array):
    return pltpu.roll(array, HD, array.ndim - 1)


def block_ranks(mask):
    blocks = mask.shape[1]
    used = jnp.max(mask.astype(jnp.float32), axis=0, keepdims=True)
    earlier = lax.broadcasted_iota(jnp.int32, (blocks, blocks), 0)
    later = lax.broadcasted_iota(jnp.int32, (blocks, blocks), 1)
    counts = ((earlier >> BAND_BITS) == (later >> BAND_BITS)) & (earlier < later)
    rank = dot_f32(jnp.broadcast_to(used, (8, blocks)).astype(jnp.bfloat16), counts.astype(jnp.float32).astype(jnp.bfloat16))
    return jnp.broadcast_to(used, (8, blocks)), rank


def slots_of(used, rank, band):
    lane = lax.broadcasted_iota(jnp.int32, used.shape, 1)
    slot = lax.broadcasted_iota(jnp.int32, used.shape, 0).astype(jnp.float32)
    return jnp.where(((lane >> BAND_BITS) == band) & (rank == slot), used, 0.0)


def project_kv(block_mask, tokens, w_key, w_value):
    pairs = w_key.shape[1] // LANES
    rows = KEEP * BLK
    step = 2 * BLK
    steps = tokens.shape[1] // step

    def kernel(mask_any, tok_ref, wk_ref, wv_ref, *rest):
        outs, own_ref, rest = rest[: pairs + 1], rest[pairs + 1], rest[pairs + 2 :]
        (mask_ref, tok, wk, wv, keys, values, held, sems, out_sems) = rest
        load_mask = pltpu.make_async_copy(mask_any, mask_ref, sems.at[0])
        load_mask.start()
        loads = []
        for c in range(steps):
            at = pl.ds(c * step, step)
            loads += [
                pltpu.make_async_copy(wk_ref.at[at, :], wk.at[at, :], sems.at[1 + 3 * c]),
                pltpu.make_async_copy(wv_ref.at[at, :], wv.at[at, :], sems.at[2 + 3 * c]),
                pltpu.make_async_copy(tok_ref.at[:, at], tok.at[:, at], sems.at[3 + 3 * c]),
            ]
        for copy in loads:
            copy.start()
        load_mask.wait()
        used, rank = block_ranks(mask_ref[...])
        picked = slots_of(used, rank, lax.axis_index("band"))
        place = (lax.broadcasted_iota(jnp.int32, picked.shape, 1) & (2**BAND_BITS - 1)).astype(jnp.float32)
        digit = lax.broadcasted_iota(jnp.int32, picked.shape, 0)
        scale = (1 << (BAND_BITS * jnp.minimum(digit, KEEP))).astype(jnp.float32)
        code = jnp.sum(jnp.where(digit < KEEP, picked * place * scale, 0.0)).astype(jnp.int32)
        low = low_lanes((rows, LANES))
        begins = [pl.multiple_of(((code >> (BAND_BITS * e)) & (2**BAND_BITS - 1)) * BLK, BLK) for e in range(KEEP)]
        for c in range(steps):
            at = pl.ds(c * step, step)
            for copy in loads[3 * c : 3 * c + 3]:
                copy.wait()
            chosen = jnp.concatenate([tok[pl.ds(begin, BLK), at] for begin in begins], axis=0)
            for total, weight in ((keys, wk), (values, wv)):
                product = dot_f32(chosen, weight[at, :])
                if c == 0:
                    total[...] = product
                else:
                    total[...] += product
        for p in range(pairs):
            cols = slice(p * LANES, (p + 1) * LANES)
            k, v = keys[:, cols], values[:, cols]
            held[p, 0] = jnp.where(low, k, swap_halves(v)).astype(jnp.bfloat16)
            held[p, 1] = jnp.where(low, swap_halves(k), v).astype(jnp.bfloat16)
        moves = [(held.at[0, 0], outs[0]), (held.at[0, 1], outs[1]), (held.at[0], own_ref)]
        moves += [(held.at[p], outs[p + 1]) for p in range(1, pairs)]
        stores = [pltpu.make_async_copy(source, to, out_sems.at[i]) for i, (source, to) in enumerate(moves)]
        for copy in stores:
            copy.start()
        for copy in stores:
            copy.wait()

    return pl.pallas_call(
        kernel,
        out_shape=[jax.ShapeDtypeStruct((rows, LANES), jnp.bfloat16)] * 2
        + [jax.ShapeDtypeStruct((2, rows, LANES), jnp.bfloat16)] * pairs,
        in_specs=[ANY] * 4,
        out_specs=[ANY] * (pairs + 2),
        scratch_shapes=[
            pltpu.VMEM(block_mask.shape, jnp.int32),
            pltpu.VMEM(tokens.shape, jnp.bfloat16),
            pltpu.VMEM(w_key.shape, jnp.bfloat16),
            pltpu.VMEM(w_value.shape, jnp.bfloat16),
            pltpu.VMEM((rows, w_key.shape[1]), jnp.float32),
            pltpu.VMEM((rows, w_key.shape[1]), jnp.float32),
            pltpu.VMEM((pairs, 2, rows, LANES), jnp.bfloat16),
            pltpu.SemaphoreType.DMA((1 + 3 * steps,)),
            pltpu.SemaphoreType.DMA((pairs + 2,)),
        ],
        compiler_params=LARGE,
        cost_estimate=FREE,
        name="project_kv",
    )(block_mask, tokens, w_key, w_value)


class Tables:
    def __init__(self, landing, key_tab, value_tab, sems, refs):
        self.landing, self.key_tab, self.value_tab = landing, key_tab, value_tab
        self.copies, taken = [], 0
        for s, ref in enumerate(refs):
            at = pl.ds(taken // 2 * HELD, HELD)
            to = landing.at[taken % 2, at, :] if len(ref.shape) == 2 else landing.at[:, at, :]
            taken += len(ref.shape) - 1
            self.copies.append((taken, pltpu.make_async_copy(ref, to, sems.at[s])))
        for _, copy in self.copies:
            copy.start()

    def fill(self, bias_ref, first):
        low = low_lanes((BLK, LANES)).astype(jnp.float32).astype(jnp.bfloat16)
        high = (1.0 - low_lanes((BLK, LANES)).astype(jnp.float32)).astype(jnp.bfloat16)
        sources = self.landing.shape[1] // HELD
        for s in range(sources):
            for taken, copy in self.copies:
                if 2 * s < taken <= 2 * s + 2:
                    copy.wait()
            for e in range(KEEP):
                at = pl.ds((s * KEEP + e) * BLK, BLK)
                row = (first + s) * 8 + e
                add = jnp.broadcast_to(bias_ref[row : row + 1, :], (BLK, LANES)).astype(jnp.bfloat16)
                for h in range(2):
                    kv = self.landing[h, at, :]
                    self.key_tab[h, at, :] = kv * low + add
                    self.value_tab[h, at, :] = kv * high + low

    def sweep(self, q, h, peak, total_sum):
        def chunk(begin, carried):
            peak, total_sum = carried
            at = pl.ds(begin, CHUNK)
            scores = lax.dot_general(
                q, self.key_tab[h, at, :], (((1,), (1,)), ((), ())), preferred_element_type=jnp.float32
            )
            new_peak = jnp.maximum(peak, jnp.max(scores, axis=1, keepdims=True))
            weights = jnp.exp2(scores - new_peak).astype(jnp.bfloat16)
            total_sum = total_sum * jnp.exp2(peak - new_peak) + dot_f32(weights, self.value_tab[h, at, :])
            return new_peak, total_sum

        def group(g, carried):
            for c in range(GROUP):
                begin = (g * GROUP + c) * CHUNK
                carried = chunk(begin if isinstance(g, int) else pl.multiple_of(begin, CHUNK), carried)
            return carried

        groups = self.key_tab.shape[1] // (GROUP * CHUNK)
        carried = (peak, total_sum)
        if groups > 2:
            return lax.fori_loop(0, groups, group, carried)
        for g in range(groups):
            carried = group(g, carried)
        return carried


def table_scratch(arrays):
    sources = sum(array.ndim - 1 for array in arrays) // 2
    table = pltpu.VMEM((2, sources * HELD, LANES), jnp.bfloat16)
    return [table, table, table, pltpu.SemaphoreType.DMA((len(arrays),))]


def begin_attention(block_mask, tokens, w_query, early, parts, source_bands):
    rows, width = tokens.shape
    pairs = w_query.shape[1] // LANES
    part = rows // parts
    per_band = rows // BLK
    key_blocks = block_mask.shape[1]
    sources = len(source_bands(0))

    def kernel(mask_ref, tok, w_any, *rest):
        early_refs, rest = rest[: len(early)], rest[len(early) :]
        outs = rest[:pairs]
        bias_ref, state_ref, held, own_rows, w, w_sem, out_sems, *scratch = rest[pairs:]
        load_w = pltpu.make_async_copy(w_any, w, w_sem)
        load_w.start()
        tables = Tables(*scratch, early_refs)
        me, band = lax.axis_index("head"), lax.axis_index("band")
        own_rows[...] = jnp.zeros(own_rows.shape, jnp.float32)
        first = pl.multiple_of(band * per_band, per_band)
        own_rows[HD : HD + per_band, :] = mask_ref[pl.ds(first, per_band), :].astype(jnp.float32)
        used, rank = block_ranks(mask_ref[...])
        lane8 = lax.broadcasted_iota(jnp.int32, (8, LANES), 1)
        for s, source in enumerate(source_bands(band)):
            allowed = lax.dot_general(
                slots_of(used, rank, source).astype(jnp.bfloat16),
                own_rows[...].astype(jnp.bfloat16),
                (((1,), (1,)), ((), ())),
                preferred_element_type=jnp.float32,
            )
            queried = (lane8 >= HD) & (lane8 < HD + per_band)
            bias_ref[s * 8 : (s + 1) * 8, :] = jnp.where(queried & (allowed < 0.5), NEG, 0.0)
        load_w.wait()
        lane = lax.broadcasted_iota(jnp.int32, (part, LANES), 1)
        row = lax.broadcasted_iota(jnp.int32, (part, LANES), 0)
        stores = []
        for k in range(parts):
            at = pl.ds(k * part, part)
            begin = pl.multiple_of((me ^ k) * part, part)
            q = dot_f32(tok[pl.ds(begin, part), :], w[...]) * QUERY_SCALE
            hot = (lane - HD == ((row + begin) >> BLK_BITS)).astype(jnp.float32)
            for p in range(pairs):
                pair = q[:, p * LANES : (p + 1) * LANES]
                held[p, 0, at, :] = jnp.where(lane < HD, pair, hot).astype(jnp.bfloat16)
                held[p, 1, at, :] = jnp.where(lane < HD, swap_halves(pair), hot).astype(jnp.bfloat16)
        for p in range(pairs):
            copy = pltpu.make_async_copy(held.at[p], outs[p], out_sems.at[p])
            copy.start()
            stores.append(copy)
        tables.fill(bias_ref, 0)
        lane = lax.broadcasted_iota(jnp.int32, (rows, LANES), 1)
        for h in range(2):
            peak, total_sum = tables.sweep(
                held[0, h], h, jnp.full((rows, 1), LOWEST, jnp.float32), jnp.zeros((rows, LANES), jnp.float32)
            )
            state_ref[h] = jnp.where(lane == 1, peak, total_sum)
        for copy in stores:
            copy.wait()

    out = pl.pallas_call(
        kernel,
        out_shape=[jax.ShapeDtypeStruct((2, rows, LANES), jnp.bfloat16)] * pairs
        + [jax.ShapeDtypeStruct((sources * 8, LANES), jnp.float32), jax.ShapeDtypeStruct((2, rows, LANES), jnp.float32)],
        in_specs=[VMEM] * 2 + [HBM] * (1 + len(early)),
        out_specs=[ANY] * pairs + [VMEM] * 2,
        scratch_shapes=[
            pltpu.VMEM((pairs, 2, rows, LANES), jnp.bfloat16),
            pltpu.VMEM((LANES, key_blocks), jnp.float32),
            pltpu.VMEM(w_query.shape, jnp.bfloat16),
            pltpu.SemaphoreType.DMA(()),
            pltpu.SemaphoreType.DMA((pairs,)),
        ]
        + table_scratch(early),
        compiler_params=PARAMS,
        cost_estimate=FREE,
        name="begin_attention",
    )(block_mask, tokens, w_query, *early)
    return out[:pairs], out[pairs], out[pairs + 1]


def attend(queries, state, sources, bias, first, parts, begin, count, cost):
    part = queries.shape[1] // parts
    rows = count * part
    states = [] if state is None else [state]

    def kernel(q_ref, bias_ref, *rest):
        state_refs, rest = rest[: len(states)], rest[len(states) :]
        srcs, rest = rest[: len(sources)], rest[len(sources) :]
        outs, scratch = rest[:count], rest[count:]
        tables = Tables(*scratch, srcs)
        tables.fill(bias_ref, first)
        lane = lax.broadcasted_iota(jnp.int32, (rows, LANES), 1)
        low = lane < HD
        taken = slice(begin * part, begin * part + rows)
        sums = []
        for h in range(2):
            if states:
                total_sum = state_refs[0][h, taken]
                peak = jnp.max(jnp.where(lane == 1, total_sum, LOWEST), axis=1, keepdims=True)
                total_sum = jnp.where(lane == 1, pltpu.roll(total_sum, 1, 1), total_sum)
            else:
                peak = jnp.full((rows, 1), LOWEST, jnp.float32)
                total_sum = jnp.zeros((rows, LANES), jnp.float32)
            sums.append(tables.sweep(q_ref[h, taken], h, peak, total_sum)[1])
        top = jnp.where(low, swap_halves(sums[0]), sums[1])
        mass = jnp.where(low, sums[0], swap_halves(sums[1]))
        out = (top / mass).astype(jnp.bfloat16)
        for k in range(count):
            outs[k][...] = out[k * part : (k + 1) * part, :]

    return pl.pallas_call(
        kernel,
        out_shape=[jax.ShapeDtypeStruct((part, LANES), jnp.bfloat16)] * count,
        in_specs=[VMEM, VMEM] + [VMEM] * len(states) + [HBM] * len(sources),
        out_specs=[VMEM] * count,
        scratch_shapes=table_scratch(sources),
        compiler_params=PARAMS,
        cost_estimate=pl.CostEstimate(flops=cost, bytes_accessed=0, transcendentals=0),
        name="attend",
    )(queries, bias, *states, *sources)


def project_out(attended, w_out, w_mine, w_other, tiles):
    depth, width = w_mine.shape[1:]
    heads, pairs = len(attended), len(attended[0])
    rows = attended[0][0].shape[0]
    piece = depth // tiles
    order = [0]
    bit = heads // 2
    while bit:
        order += [bit ^ k for k in order]
        bit //= 2
    pieces = [attended[k][p] for k in order for p in range(pairs)]
    direct = depth % LANES == 0

    def kernel(*rest):
        refs, (own_ref, mine_ref, other_ref, out_ref, *scratch) = rest[: heads * pairs], rest[heads * pairs :]
        if not direct:
            w, sems = scratch
            copies = [
                pltpu.make_async_copy(ref, w.at[:, pl.ds(s * depth, depth), :], sems.at[s])
                for s, ref in enumerate((mine_ref, other_ref))
            ]
            for copy in copies:
                copy.start()
        quarter = (lax.axis_index("band") & 1) * tiles + lax.axis_index("tiles")
        lane = lax.broadcasted_iota(jnp.int32, (rows, LANES), 1)
        groups = []
        for i in range(1, heads):
            group = [refs[i * pairs + p][...].astype(jnp.float32) for p in range(pairs)]
            size = piece
            while size < depth * 2:
                flip = (quarter & (size // piece)) > 0
                if size < LANES:
                    moved = [
                        jnp.where((lane & size) > 0, pltpu.roll(x, size, 1), pltpu.roll(x, LANES - size, 1)) for x in group
                    ]
                else:
                    moved = [group[p ^ (size // LANES)] for p in range(pairs)]
                group = [jnp.where(flip, m, x) for m, x in zip(moved, group)]
                size *= 2
            groups.append([x.astype(jnp.bfloat16) for x in group])
        total = dot_f32(jnp.concatenate([ref[...] for ref in refs[:pairs]], axis=1), own_ref[...])
        if direct:
            half = depth // LANES
            near_cols = jnp.concatenate([x for group in groups for x in group[:half]], axis=1)
            far_cols = jnp.concatenate([x for group in groups for x in group[half:]], axis=1)
            total += dot_f32(near_cols, mine_ref[...].reshape((heads - 1) * depth, width))
            total += dot_f32(far_cols, other_ref[...].reshape((heads - 1) * depth, width))
        else:
            for copy in copies:
                copy.wait()
            cols = jnp.concatenate([x for group in groups for x in group], axis=1)
            total += dot_f32(cols, w[...].reshape((heads - 1) * 2 * depth, width))
        out_ref[...] = total.astype(jnp.bfloat16)

    scratch = [pltpu.VMEM((heads - 1, 2 * depth, width), jnp.bfloat16), pltpu.SemaphoreType.DMA((2,))]
    return pl.pallas_call(
        kernel,
        out_shape=jax.ShapeDtypeStruct((rows, width), jnp.bfloat16),
        in_specs=[VMEM] * (len(pieces) + 1) + [VMEM if direct else ANY] * 2,
        out_specs=VMEM,
        scratch_shapes=[] if direct else scratch,
        compiler_params=SMALL,
        cost_estimate=FREE,
        name="project_out",
    )(*pieces, w_out, w_mine, w_other)


def on_device(sizes, tokens, w_query, w_key, w_value, w_out, block_mask):
    tiles, bands, heads = sizes
    hops = range(1, bands // 2)

    def along_band(array, goes_to):
        return lax.ppermute(array, "band", [(i, goes_to(i)) for i in range(bands)])

    def to_sibling(array):
        return along_band(array, lambda i: i ^ 1)

    def along_head(array, k):
        return lax.ppermute(array, "head", [(i, i ^ k) for i in range(heads)])

    def source_bands(band):
        found = [band, band ^ 1]
        for r in hops:
            far = lax.rem(band + bands - 2 * r, bands)
            found += [far, far ^ 1]
        return found

    kv = project_kv(block_mask, tokens, w_key, w_value)
    *kv, own = kv
    kv = [list(kv[:2])] + [[one] for one in kv[2:]]
    pairs = len(kv)
    far = [[[along_band(one, lambda i: (i + 2 * r) % bands) for one in arrays] for r in hops] for arrays in kv]
    near = [[to_sibling(one) for one in arrays] for arrays in kv]

    def widen(held, came, k):
        held = jnp.concatenate([held, came]) if came is not None else held
        return held, along_head(held, k)

    def other_tiles(array):
        return [lax.ppermute(array, "tiles", [(i, i ^ s) for i in range(tiles)]) for s in range(1, tiles)]

    quarter = (lax.axis_index("band") & 1) * tiles + lax.axis_index("tiles")
    piece = w_out.shape[0] // (2 * tiles)
    w_mine = lax.dynamic_slice_in_dim(w_out, quarter * piece, piece, 0)
    w_mine, kv = lax.optimization_barrier((w_mine, kv))
    bit = heads // 2
    w_mine, arriving = widen(w_mine[None], None, bit)
    queries, bias, state = begin_attention(block_mask, tokens, w_query, [own] + near[0], heads, source_bands)
    far[0], queries, arriving = lax.optimization_barrier((far[0], queries, arriving))
    while bit > 1:
        bit //= 2
        w_mine, arriving = widen(w_mine, arriving, bit)

    attended = [[] for _ in range(heads)]

    def exchange(pieces, first):
        for k, piece in enumerate(pieces, first):
            attended[k].append(piece if k == 0 else along_head(piece, k))

    last = pairs - 1
    if last == 0:
        w_mine = jnp.concatenate([w_mine, arriving])[1:]
        arriving = other_tiles(w_mine)
    for p in range(pairs):
        if p > 0:
            far[p], pieces = lax.optimization_barrier((far[p], pieces))
        sources = [] if p == 0 else kv[p] + near[p]
        for arrays in far[p]:
            sources += arrays + [to_sibling(one) for one in arrays]
        held, first = (state, 2) if p == 0 else (None, 0)
        if p < last:
            pieces = attend(queries[p], held, sources, bias, first, heads, 0, heads, 2**29)
            if p == 0:
                pieces, arriving = lax.optimization_barrier((pieces, arriving))
                w_mine = jnp.concatenate([w_mine, arriving])[1:]
                arriving = other_tiles(w_mine)
            exchange(pieces, 0)
        else:
            pieces = attend(queries[p], held, sources, bias, first, heads, 1, heads - 1, 2**31)
            pieces, attended, sources[-1] = lax.optimization_barrier((pieces, attended, sources[-1]))
            exchange(pieces, 1)
            arriving, sources[-1] = lax.optimization_barrier((arriving, sources[-1]))
            exchange(attend(queries[p], held, sources, bias, first, heads, 0, 1, LONG), 0)
    w_mine = jnp.concatenate([w_mine] + arriving, axis=1)
    return project_out(attended, w_out, w_mine, to_sibling(w_mine), tiles)


def solution(mesh):
    sizes = tuple(mesh.shape[axis] for axis in ("tiles", "band", "head"))
    return jax.shard_map(
        functools.partial(on_device, sizes),
        mesh=mesh,
        in_specs=(
            P(("tiles", "band"), None),
            P(None, "head"),
            P(None, "head"),
            P(None, "head"),
            P("head", None),
            P("tiles", None),
        ),
        out_specs=P(("tiles", "band", "head"), None),
        check_vma=False,
    )
```

```python
import functools
import math

import jax
import jax.numpy as jnp
from jax import lax
from jax.experimental import pallas as pl
from jax.experimental.pallas import tpu as pltpu
from jax.sharding import PartitionSpec as P

HD = 64
BLK = 128
KEEP = 6
LANES = 128
NEG = -1e30
LOWEST = -3e38
HELD = KEEP * BLK
CHUNK = 1536
LONG = 2**33
GROUP = 2 * HELD // CHUNK
QUERY_SCALE = HD**-0.5 * math.log2(math.e)
BLK_BITS = 7
BAND_BITS = 3
SMALL = pltpu.CompilerParams(vmem_limit_bytes=16 * 2**20)
FREE = pl.CostEstimate(flops=0, bytes_accessed=0, transcendentals=0)
LARGE = pltpu.CompilerParams(vmem_limit_bytes=60 * 2**20)
PARAMS = pltpu.CompilerParams(vmem_limit_bytes=32 * 2**20)
ANY = pl.BlockSpec(memory_space=pl.ANY)
HBM = pl.BlockSpec(memory_space=pltpu.HBM)
VMEM = pl.BlockSpec(memory_space=pltpu.VMEM)


def dot_f32(left, right):
    return jnp.dot(left, right, preferred_element_type=jnp.float32)


def low_lanes(shape):
    return lax.broadcasted_iota(jnp.int32, shape, len(shape) - 1) < HD


def swap_halves(array):
    return pltpu.roll(array, HD, array.ndim - 1)


def block_ranks(mask):
    blocks = mask.shape[1]
    used = jnp.max(mask.astype(jnp.float32), axis=0, keepdims=True)
    earlier = lax.broadcasted_iota(jnp.int32, (blocks, blocks), 0)
    later = lax.broadcasted_iota(jnp.int32, (blocks, blocks), 1)
    counts = ((earlier >> BAND_BITS) == (later >> BAND_BITS)) & (earlier < later)
    rank = dot_f32(jnp.broadcast_to(used, (8, blocks)).astype(jnp.bfloat16), counts.astype(jnp.float32).astype(jnp.bfloat16))
    return jnp.broadcast_to(used, (8, blocks)), rank


def slots_of(used, rank, band):
    lane = lax.broadcasted_iota(jnp.int32, used.shape, 1)
    slot = lax.broadcasted_iota(jnp.int32, used.shape, 0).astype(jnp.float32)
    return jnp.where(((lane >> BAND_BITS) == band) & (rank == slot), used, 0.0)


def project_kv(block_mask, tokens, w_key, w_value):
    pairs = w_key.shape[1] // LANES
    rows = KEEP * BLK
    step = 2 * BLK
    steps = tokens.shape[1] // step

    def kernel(mask_any, tok_ref, wk_ref, wv_ref, *rest):
        outs, own_ref, rest = rest[: pairs + 1], rest[pairs + 1], rest[pairs + 2 :]
        (mask_ref, tok, wk, wv, keys, values, held, sems, out_sems) = rest
        load_mask = pltpu.make_async_copy(mask_any, mask_ref, sems.at[0])
        load_mask.start()
        loads = []
        for c in range(steps):
            at = pl.ds(c * step, step)
            loads += [
                pltpu.make_async_copy(wk_ref.at[at, :], wk.at[at, :], sems.at[1 + 3 * c]),
                pltpu.make_async_copy(wv_ref.at[at, :], wv.at[at, :], sems.at[2 + 3 * c]),
                pltpu.make_async_copy(tok_ref.at[:, at], tok.at[:, at], sems.at[3 + 3 * c]),
            ]
        for copy in loads:
            copy.start()
        load_mask.wait()
        used, rank = block_ranks(mask_ref[...])
        picked = slots_of(used, rank, lax.axis_index("band"))
        place = (lax.broadcasted_iota(jnp.int32, picked.shape, 1) & (2**BAND_BITS - 1)).astype(jnp.float32)
        digit = lax.broadcasted_iota(jnp.int32, picked.shape, 0)
        scale = (1 << (BAND_BITS * jnp.minimum(digit, KEEP))).astype(jnp.float32)
        code = jnp.sum(jnp.where(digit < KEEP, picked * place * scale, 0.0)).astype(jnp.int32)
        low = low_lanes((rows, LANES))
        begins = [pl.multiple_of(((code >> (BAND_BITS * e)) & (2**BAND_BITS - 1)) * BLK, BLK) for e in range(KEEP)]
        for c in range(steps):
            at = pl.ds(c * step, step)
            for copy in loads[3 * c : 3 * c + 3]:
                copy.wait()
            chosen = jnp.concatenate([tok[pl.ds(begin, BLK), at] for begin in begins], axis=0)
            for total, weight in ((keys, wk), (values, wv)):
                product = dot_f32(chosen, weight[at, :])
                if c == 0:
                    total[...] = product
                else:
                    total[...] += product
        for p in range(pairs):
            cols = slice(p * LANES, (p + 1) * LANES)
            k, v = keys[:, cols], values[:, cols]
            held[p, 0] = jnp.where(low, k, swap_halves(v)).astype(jnp.bfloat16)
            held[p, 1] = jnp.where(low, swap_halves(k), v).astype(jnp.bfloat16)
        moves = [(held.at[0, 0], outs[0]), (held.at[0, 1], outs[1]), (held.at[0], own_ref)]
        moves += [(held.at[p], outs[p + 1]) for p in range(1, pairs)]
        stores = [pltpu.make_async_copy(source, to, out_sems.at[i]) for i, (source, to) in enumerate(moves)]
        for copy in stores:
            copy.start()
        for copy in stores:
            copy.wait()

    return pl.pallas_call(
        kernel,
        out_shape=[jax.ShapeDtypeStruct((rows, LANES), jnp.bfloat16)] * 2
        + [jax.ShapeDtypeStruct((2, rows, LANES), jnp.bfloat16)] * pairs,
        in_specs=[ANY] * 4,
        out_specs=[ANY] * (pairs + 2),
        scratch_shapes=[
            pltpu.VMEM(block_mask.shape, jnp.int32),
            pltpu.VMEM(tokens.shape, jnp.bfloat16),
            pltpu.VMEM(w_key.shape, jnp.bfloat16),
            pltpu.VMEM(w_value.shape, jnp.bfloat16),
            pltpu.VMEM((rows, w_key.shape[1]), jnp.float32),
            pltpu.VMEM((rows, w_key.shape[1]), jnp.float32),
            pltpu.VMEM((pairs, 2, rows, LANES), jnp.bfloat16),
            pltpu.SemaphoreType.DMA((1 + 3 * steps,)),
            pltpu.SemaphoreType.DMA((pairs + 2,)),
        ],
        compiler_params=LARGE,
        cost_estimate=FREE,
        name="project_kv",
    )(block_mask, tokens, w_key, w_value)


class Tables:
    def __init__(self, landing, key_tab, value_tab, sems, refs):
        self.landing, self.key_tab, self.value_tab = landing, key_tab, value_tab
        self.copies, taken = [], 0
        for s, ref in enumerate(refs):
            at = pl.ds(taken // 2 * HELD, HELD)
            to = landing.at[taken % 2, at, :] if len(ref.shape) == 2 else landing.at[:, at, :]
            taken += len(ref.shape) - 1
            self.copies.append((taken, pltpu.make_async_copy(ref, to, sems.at[s])))
        for _, copy in self.copies:
            copy.start()

    def fill(self, bias_ref, first):
        low = low_lanes((BLK, LANES)).astype(jnp.float32).astype(jnp.bfloat16)
        high = (1.0 - low_lanes((BLK, LANES)).astype(jnp.float32)).astype(jnp.bfloat16)
        sources = self.landing.shape[1] // HELD
        for s in range(sources):
            for taken, copy in self.copies:
                if 2 * s < taken <= 2 * s + 2:
                    copy.wait()
            for e in range(KEEP):
                at = pl.ds((s * KEEP + e) * BLK, BLK)
                row = (first + s) * 8 + e
                add = jnp.broadcast_to(bias_ref[row : row + 1, :], (BLK, LANES)).astype(jnp.bfloat16)
                for h in range(2):
                    kv = self.landing[h, at, :]
                    self.key_tab[h, at, :] = kv * low + add
                    self.value_tab[h, at, :] = kv * high + low

    def sweep(self, q, h, peak, total_sum):
        def chunk(begin, carried):
            peak, total_sum = carried
            at = pl.ds(begin, CHUNK)
            scores = lax.dot_general(
                q, self.key_tab[h, at, :], (((1,), (1,)), ((), ())), preferred_element_type=jnp.float32
            )
            new_peak = jnp.maximum(peak, jnp.max(scores, axis=1, keepdims=True))
            weights = jnp.exp2(scores - new_peak).astype(jnp.bfloat16)
            total_sum = total_sum * jnp.exp2(peak - new_peak) + dot_f32(weights, self.value_tab[h, at, :])
            return new_peak, total_sum

        def group(g, carried):
            for c in range(GROUP):
                begin = (g * GROUP + c) * CHUNK
                carried = chunk(begin if isinstance(g, int) else pl.multiple_of(begin, CHUNK), carried)
            return carried

        groups = self.key_tab.shape[1] // (GROUP * CHUNK)
        carried = (peak, total_sum)
        if groups > 2:
            return lax.fori_loop(0, groups, group, carried)
        for g in range(groups):
            carried = group(g, carried)
        return carried


def table_scratch(arrays):
    sources = sum(array.ndim - 1 for array in arrays) // 2
    table = pltpu.VMEM((2, sources * HELD, LANES), jnp.bfloat16)
    return [table, table, table, pltpu.SemaphoreType.DMA((len(arrays),))]


def begin_attention(block_mask, tokens, w_query, early, parts, source_bands):
    rows, width = tokens.shape
    pairs = w_query.shape[1] // LANES
    part = rows // parts
    per_band = rows // BLK
    key_blocks = block_mask.shape[1]
    sources = len(source_bands(0))

    def kernel(mask_ref, tok, w_any, *rest):
        early_refs, rest = rest[: len(early)], rest[len(early) :]
        outs = rest[:pairs]
        bias_ref, state_ref, held, own_rows, w, w_sem, out_sems, *scratch = rest[pairs:]
        load_w = pltpu.make_async_copy(w_any, w, w_sem)
        load_w.start()
        tables = Tables(*scratch, early_refs)
        me, band = lax.axis_index("head"), lax.axis_index("band")
        own_rows[...] = jnp.zeros(own_rows.shape, jnp.float32)
        first = pl.multiple_of(band * per_band, per_band)
        own_rows[HD : HD + per_band, :] = mask_ref[pl.ds(first, per_band), :].astype(jnp.float32)
        used, rank = block_ranks(mask_ref[...])
        lane8 = lax.broadcasted_iota(jnp.int32, (8, LANES), 1)
        for s, source in enumerate(source_bands(band)):
            allowed = lax.dot_general(
                slots_of(used, rank, source).astype(jnp.bfloat16),
                own_rows[...].astype(jnp.bfloat16),
                (((1,), (1,)), ((), ())),
                preferred_element_type=jnp.float32,
            )
            queried = (lane8 >= HD) & (lane8 < HD + per_band)
            bias_ref[s * 8 : (s + 1) * 8, :] = jnp.where(queried & (allowed < 0.5), NEG, 0.0)
        load_w.wait()
        lane = lax.broadcasted_iota(jnp.int32, (part, LANES), 1)
        row = lax.broadcasted_iota(jnp.int32, (part, LANES), 0)
        stores = []
        for k in range(parts):
            at = pl.ds(k * part, part)
            begin = pl.multiple_of((me ^ k) * part, part)
            q = dot_f32(tok[pl.ds(begin, part), :], w[...]) * QUERY_SCALE
            hot = (lane - HD == ((row + begin) >> BLK_BITS)).astype(jnp.float32)
            for p in range(pairs):
                pair = q[:, p * LANES : (p + 1) * LANES]
                held[p, 0, at, :] = jnp.where(lane < HD, pair, hot).astype(jnp.bfloat16)
                held[p, 1, at, :] = jnp.where(lane < HD, swap_halves(pair), hot).astype(jnp.bfloat16)
        for p in range(pairs):
            copy = pltpu.make_async_copy(held.at[p], outs[p], out_sems.at[p])
            copy.start()
            stores.append(copy)
        tables.fill(bias_ref, 0)
        lane = lax.broadcasted_iota(jnp.int32, (rows, LANES), 1)
        for h in range(2):
            peak, total_sum = tables.sweep(
                held[0, h], h, jnp.full((rows, 1), LOWEST, jnp.float32), jnp.zeros((rows, LANES), jnp.float32)
            )
            state_ref[h] = jnp.where(lane == 1, peak, total_sum)
        for copy in stores:
            copy.wait()

    out = pl.pallas_call(
        kernel,
        out_shape=[jax.ShapeDtypeStruct((2, rows, LANES), jnp.bfloat16)] * pairs
        + [jax.ShapeDtypeStruct((sources * 8, LANES), jnp.float32), jax.ShapeDtypeStruct((2, rows, LANES), jnp.float32)],
        in_specs=[VMEM] * 2 + [HBM] * (1 + len(early)),
        out_specs=[ANY] * pairs + [VMEM] * 2,
        scratch_shapes=[
            pltpu.VMEM((pairs, 2, rows, LANES), jnp.bfloat16),
            pltpu.VMEM((LANES, key_blocks), jnp.float32),
            pltpu.VMEM(w_query.shape, jnp.bfloat16),
            pltpu.SemaphoreType.DMA(()),
            pltpu.SemaphoreType.DMA((pairs,)),
        ]
        + table_scratch(early),
        compiler_params=PARAMS,
        cost_estimate=FREE,
        name="begin_attention",
    )(block_mask, tokens, w_query, *early)
    return out[:pairs], out[pairs], out[pairs + 1]


def attend(queries, state, sources, bias, first, parts, begin, count, cost):
    part = queries.shape[1] // parts
    rows = count * part
    states = [] if state is None else [state]

    def kernel(q_ref, bias_ref, *rest):
        state_refs, rest = rest[: len(states)], rest[len(states) :]
        srcs, rest = rest[: len(sources)], rest[len(sources) :]
        outs, scratch = rest[:count], rest[count:]
        tables = Tables(*scratch, srcs)
        tables.fill(bias_ref, first)
        lane = lax.broadcasted_iota(jnp.int32, (rows, LANES), 1)
        low = lane < HD
        taken = slice(begin * part, begin * part + rows)
        sums = []
        for h in range(2):
            if states:
                total_sum = state_refs[0][h, taken]
                peak = jnp.max(jnp.where(lane == 1, total_sum, LOWEST), axis=1, keepdims=True)
                total_sum = jnp.where(lane == 1, pltpu.roll(total_sum, 1, 1), total_sum)
            else:
                peak = jnp.full((rows, 1), LOWEST, jnp.float32)
                total_sum = jnp.zeros((rows, LANES), jnp.float32)
            sums.append(tables.sweep(q_ref[h, taken], h, peak, total_sum)[1])
        top = jnp.where(low, swap_halves(sums[0]), sums[1])
        mass = jnp.where(low, sums[0], swap_halves(sums[1]))
        out = (top / mass).astype(jnp.bfloat16)
        for k in range(count):
            outs[k][...] = out[k * part : (k + 1) * part, :]

    return pl.pallas_call(
        kernel,
        out_shape=[jax.ShapeDtypeStruct((part, LANES), jnp.bfloat16)] * count,
        in_specs=[VMEM, VMEM] + [VMEM] * len(states) + [HBM] * len(sources),
        out_specs=[VMEM] * count,
        scratch_shapes=table_scratch(sources),
        compiler_params=PARAMS,
        cost_estimate=pl.CostEstimate(flops=cost, bytes_accessed=0, transcendentals=0),
        name="attend",
    )(queries, bias, *states, *sources)


def project_out(attended, w_out, w_mine, w_other, tiles):
    depth, width = w_mine.shape[1:]
    heads, pairs = len(attended), len(attended[0])
    rows = attended[0][0].shape[0]
    piece = depth // tiles
    order = [0]
    bit = heads // 2
    while bit:
        order += [bit ^ k for k in order]
        bit //= 2
    pieces = [attended[k][p] for k in order for p in range(pairs)]
    direct = depth % LANES == 0

    def kernel(*rest):
        refs, (own_ref, mine_ref, other_ref, out_ref, *scratch) = rest[: heads * pairs], rest[heads * pairs :]
        if not direct:
            w, sems = scratch
            copies = [
                pltpu.make_async_copy(ref, w.at[:, pl.ds(s * depth, depth), :], sems.at[s])
                for s, ref in enumerate((mine_ref, other_ref))
            ]
            for copy in copies:
                copy.start()
        quarter = (lax.axis_index("band") & 1) * tiles + lax.axis_index("tiles")
        lane = lax.broadcasted_iota(jnp.int32, (rows, LANES), 1)
        groups = []
        for i in range(1, heads):
            group = [refs[i * pairs + p][...].astype(jnp.float32) for p in range(pairs)]
            size = piece
            while size < depth * 2:
                flip = (quarter & (size // piece)) > 0
                if size < LANES:
                    moved = [
                        jnp.where((lane & size) > 0, pltpu.roll(x, size, 1), pltpu.roll(x, LANES - size, 1)) for x in group
                    ]
                else:
                    moved = [group[p ^ (size // LANES)] for p in range(pairs)]
                group = [jnp.where(flip, m, x) for m, x in zip(moved, group)]
                size *= 2
            groups.append([x.astype(jnp.bfloat16) for x in group])
        total = dot_f32(jnp.concatenate([ref[...] for ref in refs[:pairs]], axis=1), own_ref[...])
        if direct:
            half = depth // LANES
            near_cols = jnp.concatenate([x for group in groups for x in group[:half]], axis=1)
            far_cols = jnp.concatenate([x for group in groups for x in group[half:]], axis=1)
            total += dot_f32(near_cols, mine_ref[...].reshape((heads - 1) * depth, width))
            total += dot_f32(far_cols, other_ref[...].reshape((heads - 1) * depth, width))
        else:
            for copy in copies:
                copy.wait()
            cols = jnp.concatenate([x for group in groups for x in group], axis=1)
            total += dot_f32(cols, w[...].reshape((heads - 1) * 2 * depth, width))
        out_ref[...] = total.astype(jnp.bfloat16)

    scratch = [pltpu.VMEM((heads - 1, 2 * depth, width), jnp.bfloat16), pltpu.SemaphoreType.DMA((2,))]
    return pl.pallas_call(
        kernel,
        out_shape=jax.ShapeDtypeStruct((rows, width), jnp.bfloat16),
        in_specs=[VMEM] * (len(pieces) + 1) + [VMEM if direct else ANY] * 2,
        out_specs=VMEM,
        scratch_shapes=[] if direct else scratch,
        compiler_params=SMALL,
        cost_estimate=FREE,
        name="project_out",
    )(*pieces, w_out, w_mine, w_other)


def on_device(sizes, tokens, w_query, w_key, w_value, w_out, block_mask):
    tiles, bands, heads = sizes
    hops = range(1, bands // 2)

    def along_band(array, goes_to):
        return lax.ppermute(array, "band", [(i, goes_to(i)) for i in range(bands)])

    def to_sibling(array):
        return along_band(array, lambda i: i ^ 1)

    def along_head(array, k):
        return lax.ppermute(array, "head", [(i, i ^ k) for i in range(heads)])

    def source_bands(band):
        found = [band, band ^ 1]
        for r in hops:
            far = lax.rem(band + bands - 2 * r, bands)
            found += [far, far ^ 1]
        return found

    kv = project_kv(block_mask, tokens, w_key, w_value)
    *kv, own = kv
    kv = [list(kv[:2])] + [[one] for one in kv[2:]]
    pairs = len(kv)
    far = [[[along_band(one, lambda i: (i + 2 * r) % bands) for one in arrays] for r in hops] for arrays in kv]
    near = [[to_sibling(one) for one in arrays] for arrays in kv]

    def widen(held, came, k):
        held = jnp.concatenate([held, came]) if came is not None else held
        return held, along_head(held, k)

    def other_tiles(array):
        return [lax.ppermute(array, "tiles", [(i, i ^ s) for i in range(tiles)]) for s in range(1, tiles)]

    quarter = (lax.axis_index("band") & 1) * tiles + lax.axis_index("tiles")
    piece = w_out.shape[0] // (2 * tiles)
    w_mine = lax.dynamic_slice_in_dim(w_out, quarter * piece, piece, 0)
    w_mine, kv = lax.optimization_barrier((w_mine, kv))
    bit = heads // 2
    w_mine, arriving = widen(w_mine[None], None, bit)
    queries, bias, state = begin_attention(block_mask, tokens, w_query, [own] + near[0], heads, source_bands)
    far[0], queries, arriving = lax.optimization_barrier((far[0], queries, arriving))
    while bit > 1:
        bit //= 2
        w_mine, arriving = widen(w_mine, arriving, bit)

    attended = [[] for _ in range(heads)]

    def exchange(pieces, first):
        for k, piece in enumerate(pieces, first):
            attended[k].append(piece if k == 0 else along_head(piece, k))

    last = pairs - 1
    if last == 0:
        w_mine = jnp.concatenate([w_mine, arriving])[1:]
        arriving = other_tiles(w_mine)
    for p in range(pairs):
        if p > 0:
            far[p], pieces = lax.optimization_barrier((far[p], pieces))
        sources = [] if p == 0 else kv[p] + near[p]
        for arrays in far[p]:
            sources += arrays + [to_sibling(one) for one in arrays]
        held, first = (state, 2) if p == 0 else (None, 0)
        if p < last:
            pieces = attend(queries[p], held, sources, bias, first, heads, 0, heads, 0)
            if p == 0:
                pieces, arriving = lax.optimization_barrier((pieces, arriving))
                w_mine = jnp.concatenate([w_mine, arriving])[1:]
                arriving = other_tiles(w_mine)
            exchange(pieces, 0)
        else:
            pieces = attend(queries[p], held, sources, bias, first, heads, 1, heads - 1, 3 * 2**29)
            pieces, attended, sources[-1] = lax.optimization_barrier((pieces, attended, sources[-1]))
            exchange(pieces, 1)
            arriving, sources[-1] = lax.optimization_barrier((arriving, sources[-1]))
            exchange(attend(queries[p], held, sources, bias, first, heads, 0, 1, LONG), 0)
    w_mine = jnp.concatenate([w_mine] + arriving, axis=1)
    return project_out(attended, w_out, w_mine, to_sibling(w_mine), tiles)


def solution(mesh):
    sizes = tuple(mesh.shape[axis] for axis in ("tiles", "band", "head"))
    return jax.shard_map(
        functools.partial(on_device, sizes),
        mesh=mesh,
        in_specs=(
            P(("tiles", "band"), None),
            P(None, "head"),
            P(None, "head"),
            P(None, "head"),
            P("head", None),
            P("tiles", None),
        ),
        out_specs=P(("tiles", "band", "head"), None),
        check_vma=False,
    )
```
